256 devices in a mesh: section: 8 (over y, core), dp: 32 (over z, x).
Axes of the slice: x: 4, y: 4, z: 8, core: 2. Of those that a mesh axis runs over, the one named last changes fastest.
Arguments:
- layer_inputs: bfloat16 [8, 15360, 8192], P('section', 'dp')
- key_cotangent: bfloat16 [8, 15360, 512], P('section', 'dp')
- token_counts: int32 [32, 4], P('dp'), may hold values from 30 to 120, as said below
- rollback_flags: int32 [8], replicated, may hold values from 0 to 1
- master_param: float32 [8, 8192, 512], P('section', 'dp'), may hold values from -6 to 6
- first_moment: float32 [8, 8192, 512], P('section', 'dp'), may hold values from -4 to 4
- second_moment: float32 [8, 8192, 512], P('section', 'dp'), may hold values from 0.05 to 1
Outputs:
- new_param: float32 [8, 8192, 512], P('section', 'dp')
- new_first: float32 [8, 8192, 512], P('section', 'dp')
- new_second: float32 [8, 8192, 512], P('section', 'dp')
- update_direction: float32 [8, 8192, 512], P('section', 'dp')
The draws below stay inside these ranges and needn't reach their ends.
Inputs may be any that keep to these rules, and one draw needn't show every extreme that they name: `token_counts`: each entry counts the leading token slots of its micro-batch that hold tokens; some micro-batch holds 120.
All inputs are finite; a program needn't handle non-finite values.
Results may differ from the reference program's by a relative error of at most 0.00095.
Values may be sent and summed in bfloat16 or wider, within the bound.
A program may use at most 128 MiB of HBM per device.

```python
import math
import jax
import jax.numpy as jnp
from jax import lax

D = 8192
KV = 512
TOK_DEV = 480
MB = 4
HIST = 8
MB_ROWS = 120
TOKENS = 15360
N_SECTION = 8
N_DP = 32


def draw_layer_inputs(key, part):
    key = jax.random.fold_in(key, 11)
    key_base, key_column = jax.random.split(key, 2)
    column_draw = jax.random.uniform(key_column, (D,), jnp.float32)
    rising = 1.0 + 2.0 * jnp.arange(D, dtype=jnp.float32) / (D - 1)
    column_scale = jnp.exp(column_draw * math.log(10.0)) * rising / 4.0
    base_draw = jax.random.normal(key_base, (N_SECTION, TOKENS, D), jnp.float32)
    return (base_draw * column_scale).astype(jnp.bfloat16)


def draw_key_cotangent(key, part):
    key = jax.random.fold_in(key, 12)
    key_base, key_column = jax.random.split(key, 2)
    column_draw = jax.random.uniform(key_column, (KV,), jnp.float32)
    column_scale = jnp.exp(column_draw * math.log(10.0)) / 3.0
    section_scale = 3.0 - 2.0 * jnp.arange(N_SECTION, dtype=jnp.float32) / (N_SECTION - 1)
    base_draw = jax.random.normal(key_base, (N_SECTION, TOKENS, KV), jnp.float32)
    return (base_draw * column_scale * section_scale[:, None, None]).astype(jnp.bfloat16)


def draw_token_counts(key, part):
    key = jax.random.fold_in(key, 13)
    key_fill, key_spot = jax.random.split(key)
    lowest = max(1, MB_ROWS // 4)
    filled = jax.random.randint(key_fill, (N_DP * MB,), lowest, MB_ROWS + 1)
    chosen = jax.random.randint(key_spot, (), 0, N_DP * MB)
    filled = jnp.where(jnp.arange(N_DP * MB) == chosen, MB_ROWS, filled)
    return filled.reshape(N_DP, MB).astype(jnp.int32)


def place_ends(result, rng, low, largest):
    longest = result.shape.index(max(result.shape))
    spots = []
    for shift in (0, 1):
        where = [jax.random.randint(jax.random.fold_in(rng, axis), (), 0, length) for axis, length in enumerate(result.shape)]
        where[longest] = (where[longest] + shift) % result.shape[longest]
        spots.append(tuple(where))
    return result.at[spots[0]].set(low).at[spots[1]].set(largest)


def shard_levels(key, dims, cuts, low, high):
    gain, own = 1.0, jax.random.fold_in(key, 6)
    for position, parts in cuts:
        draws = jnp.exp(jax.random.uniform(jax.random.fold_in(own, position), (parts,), jnp.float32, low / len(cuts), high / len(cuts)))
        gain = gain * jnp.repeat(draws, dims[position] // parts).reshape([-1 if axis == position else 1 for axis in range(len(dims))])
    return gain


def normal_values(stream_key, shape, spread, bound, pieces=(), kind=jnp.bfloat16):
    loudness = shard_levels(stream_key, shape, pieces, -0.22, 0.18) if pieces else 1.0
    array = jax.random.normal(stream_key, shape, jnp.float32) * spread * loudness
    return jnp.minimum(jnp.maximum(array, -bound), bound).astype(kind)


def setup_inputs(seed: int = 0) -> dict:
    key_list = jax.random.split(jax.random.key(seed), 8)
    return {
        "layer_inputs": draw_layer_inputs(jax.random.fold_in(key_list[7], 71), 0),
        "key_cotangent": draw_key_cotangent(jax.random.fold_in(key_list[7], 71), 0),
        "token_counts": draw_token_counts(jax.random.fold_in(key_list[7], 71), 0),
        "rollback_flags": place_ends(jax.random.randint(key_list[3], (HIST,), 0, 2), jax.random.fold_in(key_list[3], 1), 0, 1).astype(jnp.int32),
        "master_param": normal_values(key_list[4], (N_SECTION, D, KV), 1.0, 6.0, ((0, 8), (1, 32)), jnp.float32),
        "first_moment": normal_values(key_list[5], (N_SECTION, D, KV), 0.3, 4.0, ((0, 8), (1, 32)), jnp.float32),
        "second_moment": jnp.clip(jnp.exp(math.log(1.0) - 2.9957323 * jax.random.uniform(key_list[6], (N_SECTION, D, KV), jnp.float32) ** shard_levels(key_list[6], (N_SECTION, D, KV), ((0, 8), (1, 32)), -0.2, 0.2)), 0.05, 1.0),
    }


beta_first = 0.9
beta_second = 0.95
adam_epsilon = 1e-08
weight_decay = 0.1
learn_rate = 0.00015
clip_level = 1.0

def reference(layer_inputs, key_cotangent, token_counts, rollback_flags, master_param, first_moment, second_moment):
    slot_pos = lax.broadcasted_iota(jnp.int32, (N_DP, MB, MB_ROWS), 2)
    valid = slot_pos < token_counts[:, :, None]

    def section_gradient(inputs):
        section_rows, section_cot = inputs
        shaped = section_cot.reshape(N_DP, MB, MB_ROWS, KV)
        masked = jnp.where(valid[:, :, :, None], shaped, jnp.zeros((), section_cot.dtype)).reshape(N_DP, TOK_DEV, KV)
        blocked = section_rows.reshape(N_DP, TOK_DEV, D)

        def add_replica(running, block_pair):
            input_block, cot_block = block_pair
            partial_term = lax.dot_general(input_block, cot_block, (((0,), (0,)), ((), ())), preferred_element_type=jnp.float32)
            return (running + partial_term, None)
        summed, _ = lax.scan(add_replica, jnp.zeros((D, KV), jnp.float32), (blocked, masked))
        return summed
    gradient = lax.map(section_gradient, (layer_inputs, key_cotangent))
    total_sq = jnp.sum(gradient * gradient)
    entries = N_SECTION * D * KV
    clip_scale = clip_level * math.sqrt(entries) / (jnp.sqrt(total_sq) + 1e-06)
    clipped = gradient * clip_scale
    step_count = (1 + jnp.sum((rollback_flags == 0).astype(jnp.int32))).astype(jnp.float32)
    bias_one = 1.0 - jnp.power(jnp.float32(beta_first), step_count)
    bias_two = 1.0 - jnp.power(jnp.float32(beta_second), step_count)
    new_first = beta_first * first_moment + (1.0 - beta_first) * clipped
    new_second = beta_second * second_moment + (1.0 - beta_second) * clipped * clipped
    update_direction = new_first / bias_one / (jnp.sqrt(new_second / bias_two) + adam_epsilon) + weight_decay * master_param
    new_param = master_param - learn_rate * update_direction
    return (new_param, new_first, new_second, update_direction)
```

```python
import math

import jax
import jax.numpy as jnp
from jax import lax
from jax.experimental import pallas as pl
from jax.experimental.pallas import tpu as pltpu
from jax.sharding import PartitionSpec as P

beta_first = 0.9
beta_second = 0.95
adam_epsilon = 1e-08
weight_decay = 0.1
learn_rate = 0.00015
clip_level = 1.0

NX, NZ, NY = 4, 8, 4
MESH = pl.DeviceIdType.MESH
LIMIT = 32767.0
TINY = 1e-33

PIECES = {"A0": (0, 160), "B0": (160, 96), "A1": (256, 144), "B1": (400, 112)}
SIGN = {"A0": 1, "A1": -1, "B0": 1, "B1": -1}
STEP = {"A0": 160, "A1": 144, "B0": 96, "B1": 112}
DZ_ORDER = (4, 3, -3, 2, -2, 1, -1, 0)
DX_ORDER = (2, 1, -1, 0)

ORDER = (
    0, 32, 96, 64, 4, 1, 8, 36, 68, 100, 33, 40, 97, 2, 65, 34,
    112, 72, 104, 80, 5, 6, 69, 9, 10, 66, 76, 12, 38, 3, 35, 16,
    42, 73, 44, 84, 37, 81, 11, 48, 41, 88, 98, 7, 113, 13, 14, 101,
    105, 17, 116, 120, 18, 108, 43, 46, 39, 20, 50, 70, 24, 67, 52, 77,
    74, 45, 56, 85, 82, 49, 92, 89, 99, 102, 21, 114, 117, 22, 106, 25,
    109, 121, 26, 124, 19, 15, 28, 51, 54, 47, 53, 78, 58, 75, 57, 86,
    60, 83, 93, 71, 90, 115, 103, 118, 107, 30, 110, 122, 29, 125, 27, 23,
    79, 59, 87, 55, 61, 62, 94, 91, 111, 123, 119, 126, 31, 63, 95, 127,
)


def build_tasks():
    tasks = {}
    for c in ("A0", "A1"):
        sg = SIGN[c]
        for dz in DZ_ORDER:
            tasks[(c, "x", dz, 2 * sg)] = (c, (dz, 2), (), ("x", sg))
            tasks[(c, "x", dz, -sg)] = (c, (dz, -sg), (), ("x", -sg))
            tasks[(c, "x", dz, sg)] = (c, (dz, sg), ((c, "x", dz, 2 * sg),), ("x", sg))
            ins = [(c, "x", dz, sg), (c, "x", dz, -sg)]
            d = dz if dz != 4 else 4 * sg
            out = None
            if d == 0:
                ins += [(c, "z", sg), (c, "z", -sg)]
            else:
                s = 1 if d > 0 else -1
                if abs(d) < (4 if s == sg else 3):
                    ins.append((c, "z", d + s))
                out = ("z", s)
            tasks[(c, "z", d)] = (c, (dz, 0), tuple(ins), out)
    for c in ("B0", "B1"):
        sg = SIGN[c]
        for dx in DX_ORDER:
            for k in (4, 3, 2, 1):
                d = k * sg
                ins = () if k == 4 else ((c, "z", dx, d + sg),)
                tasks[(c, "z", dx, d)] = (c, (4 if k == 4 else d, dx), ins, ("z", sg))
            for k in (3, 2, 1):
                d = -k * sg
                ins = () if k == 3 else ((c, "z", dx, d - sg),)
                tasks[(c, "z", dx, d)] = (c, (d, dx), ins, ("z", -sg))
            ins = [(c, "z", dx, sg), (c, "z", dx, -sg)]
            out, d = None, dx
            if dx == 0:
                ins += [(c, "x", sg), (c, "x", -sg)]
            elif dx == 2:
                out, d = ("x", sg), 2 * sg
            elif dx == sg:
                ins.append((c, "x", 2 * sg))
                out = ("x", sg)
            else:
                out = ("x", -sg)
            tasks[(c, "x", d)] = (c, (0, dx), tuple(ins), out)
    return tasks


TASKS = build_tasks()
NAMES = list(TASKS)
SEQUENCE = [NAMES[i] for i in ORDER]
BLOCKS = list(dict.fromkeys(TASKS[n][1] for n in SEQUENCE))
MESSAGES = {}
for _n in SEQUENCE:
    if TASKS[_n][3] is not None:
        _c = TASKS[_n][0]
        MESSAGES[_n] = (_c, sum(1 for m in MESSAGES if MESSAGES[m][0] == _c))
N_MSG = 31
CLASSES = ("A0", "A1", "B0", "B1")
GROUP = 4


def kernel(x_hbm, m_hbm, counts, g_out, sq_out, xbuf, mbuf, masked, mt, part, tmp, grad, *rest):
    snd, rcv, hsnd, hrcv = rest[0:4], rest[4:8], rest[8:12], rest[12:16]
    ssem, rsem, hssem, hrsem, xsem, msem, red, redr0, redr1, s0, r0, s1, r1 = rest[16:]
    width = mbuf.shape[1]
    section, dp = lax.axis_index("section"), lax.axis_index("dp")
    y, core = section // 2, lax.rem(section, 2)
    z, x = dp // NX, lax.rem(dp, NX)

    def at(dz=0, dx=0, dy=0, dc=0):
        return {
            "section": lax.rem(y + dy + NY, NY) * 2 + lax.rem(core + dc, 2),
            "dp": lax.rem(z + dz + NZ, NZ) * NX + lax.rem(x + dx + NX, NX),
        }

    plane = [(0, dx, dy, 0) for dx in range(NX) for dy in range(NY) if (dx, dy) != (0, 0)]
    column = [(dz, 0, 0, dc) for dz in range(NZ) for dc in range(2) if (dz, dc) != (0, 0)]

    mload = pltpu.make_async_copy(m_hbm.at[0], mbuf, msem)
    mload.start()

    def xload(i):
        dz, dx = BLOCKS[i]
        first = (lax.rem(z + dz + NZ, NZ) * NX + lax.rem(x + dx + NX, NX)) * 256
        return pltpu.make_async_copy(
            x_hbm.at[0, :, pl.ds(pl.multiple_of(first, 256), 256)], xbuf.at[i], xsem.at[i]
        )

    for i in range(len(BLOCKS)):
        xload(i).start()

    barrier = pltpu.get_barrier_semaphore()
    peers = plane + column
    for peer in peers:
        pl.semaphore_signal(barrier, inc=1, device_id=at(*peer), device_id_type=MESH)

    mload.wait()
    per_micro = mbuf.shape[0] // counts.shape[1]
    for j in range(counts.shape[1]):
        rows = lax.broadcasted_iota(jnp.int32, (per_micro, width), 0)
        block = mbuf[j * per_micro : (j + 1) * per_micro, :].astype(jnp.float32)
        masked[j * per_micro : (j + 1) * per_micro, :] = jnp.where(rows < counts[0, j], block, 0.0)
    mt[...] = masked[...].T.astype(jnp.bfloat16)

    done = set()

    def need(block):
        if block in done:
            return
        i = BLOCKS.index(block)
        last = min(i + GROUP, len(BLOCKS))
        for j in range(i, last):
            done.add(BLOCKS[j])
            xload(j).wait()

        def dot(j, _):
            part[j] = jnp.dot(mt[...], xbuf[j], preferred_element_type=jnp.float32)
            return 0

        lax.fori_loop(i, last, dot, 0)

    def send(name):
        c, i = MESSAGES[name]
        axis, s = TASKS[name][3]
        k = CLASSES.index(c)
        to = at(dz=s) if axis == "z" else at(dx=s)
        return (
            pltpu.make_async_remote_copy(
                snd[k].at[i], rcv[k].at[i], ssem.at[k, i], rsem.at[k, i], device_id=to, device_id_type=MESH
            ),
            pltpu.make_async_remote_copy(
                hsnd[k].at[i], hrcv[k].at[i], hssem.at[k, i], hrsem.at[k, i], device_id=to, device_id_type=MESH
            ),
        )

    entered = False
    sums = jnp.zeros((8, 256), jnp.float32)
    for name in SEQUENCE:
        c, block, ins, out = TASKS[name]
        first, rows = PIECES[c]
        k, step = CLASSES.index(c), STEP[c]
        need(block)
        b = BLOCKS.index(block)
        scales = []
        for n in ins:
            data, head = send(n)
            head.wait_recv()
            data.wait_recv()
            scales.append(hrcv[k][MESSAGES[n][1]])

        def value(r, size):
            acc = part[b, pl.ds(first + r, size), :]
            for n, scale in zip(ins, scales):
                acc = acc + rcv[k][MESSAGES[n][1], pl.ds(r, size), :].astype(jnp.float32) * scale
            return acc

        if out is None:

            def final(g, total):
                acc = value(g * step, step)
                grad[pl.ds(first + g * step, step), :] = acc
                return total + jnp.sum((acc * acc).reshape(step // 8, 8, 256), axis=0)

            sums = lax.fori_loop(0, rows // step, final, sums)
            continue

        def high(g, top):
            acc = value(g * step, step)
            if ins:
                tmp[pl.ds(g * step, step), :] = acc
            return jnp.maximum(top, jnp.max(jnp.abs(acc).reshape(step // 8, 8, 256), axis=0))

        top = lax.fori_loop(0, rows // step, high, jnp.full((8, 256), TINY, jnp.float32))
        top = jnp.max(top, axis=0, keepdims=True)
        i = MESSAGES[name][1]
        hsnd[k][i] = top * (1.0 / LIMIT)
        inverse = LIMIT / top

        def narrow(g, _):
            acc = tmp[pl.ds(g * step, step), :] if ins else part[b, pl.ds(first + g * step, step), :]
            snd[k][i, pl.ds(g * step, step), :] = jnp.round(acc * inverse).astype(jnp.int16)
            return 0

        lax.fori_loop(0, rows // step, narrow, 0)
        if not entered:
            pl.semaphore_wait(barrier, len(peers))
            entered = True
        data, head = send(name)
        head.start()
        data.start()

    sums = jnp.sum(sums, axis=0, keepdims=True)
    red[0] = sums[:, :128] + sums[:, 128:]
    for q, (dirs, dst, ss, rs) in enumerate(((plane, redr0, s0, r0), (column, redr1, s1, r1))):
        for j, d in enumerate(dirs):
            pltpu.make_async_remote_copy(
                red.at[q], dst.at[j], ss, rs, device_id=at(*d), device_id_type=MESH
            ).start()
        if q == 0:
            for n in SEQUENCE:
                if TASKS[n][3] is not None:
                    data, head = send(n)
                    head.wait_send()
                    data.wait_send()
            for j in range(0, 256, 128):
                g_out[j : j + 128, :] = grad[:, j : j + 128].T
        whole = pltpu.make_async_remote_copy(dst, dst, ss, rs, device_id=at(*dirs[0]), device_id_type=MESH)
        whole.wait_recv()
        red[q + 1] = red[q] + jnp.sum(dst[...], axis=0)
        whole.wait_send()
    sq_out[...] = jnp.broadcast_to(red[2], (8, 128))


def reduced(layer_inputs, key_cotangent, token_counts):
    _, tokens, depth = layer_inputs.shape
    width = key_cotangent.shape[2]
    anywhere = pl.BlockSpec(memory_space=pl.ANY)
    vmem = pl.BlockSpec(memory_space=pltpu.VMEM)
    pieces = [PIECES[c][1] for c in CLASSES]
    return pl.pallas_call(
        kernel,
        out_shape=(
            jax.ShapeDtypeStruct((256, width), jnp.float32),
            jax.ShapeDtypeStruct((8, 128), jnp.float32),
        ),
        in_specs=[anywhere, anywhere, pl.BlockSpec(memory_space=pltpu.SMEM)],
        out_specs=(vmem, vmem),
        scratch_shapes=[
            pltpu.VMEM((32, tokens, 256), jnp.bfloat16),
            pltpu.VMEM((tokens, width), jnp.bfloat16),
            pltpu.VMEM((tokens, width), jnp.float32),
            pltpu.VMEM((width, tokens), jnp.bfloat16),
            pltpu.VMEM((32, width, 256), jnp.float32),
            pltpu.VMEM((160, 256), jnp.float32),
            pltpu.VMEM((width, 256), jnp.float32),
            *[pltpu.VMEM((N_MSG, r, 256), jnp.int16) for r in pieces],
            *[pltpu.VMEM((N_MSG, r, 256), jnp.int16) for r in pieces],
            *[pltpu.VMEM((N_MSG, 1, 256), jnp.float32) for r in pieces],
            *[pltpu.VMEM((N_MSG, 1, 256), jnp.float32) for r in pieces],
            pltpu.SemaphoreType.DMA((4, N_MSG)),
            pltpu.SemaphoreType.DMA((4, N_MSG)),
            pltpu.SemaphoreType.DMA((4, N_MSG)),
            pltpu.SemaphoreType.DMA((4, N_MSG)),
            pltpu.SemaphoreType.DMA((32,)),
            pltpu.SemaphoreType.DMA,
            pltpu.VMEM((3, 1, 128), jnp.float32),
            pltpu.VMEM((15, 1, 128), jnp.float32),
            pltpu.VMEM((15, 1, 128), jnp.float32),
            pltpu.SemaphoreType.DMA,
            pltpu.SemaphoreType.DMA,
            pltpu.SemaphoreType.DMA,
            pltpu.SemaphoreType.DMA,
        ],
        compiler_params=pltpu.CompilerParams(
            collective_id=0, has_side_effects=True, vmem_limit_bytes=56 << 20
        ),
    )(layer_inputs, key_cotangent, token_counts)


def local(
    layer_inputs,
    key_cotangent,
    token_counts,
    rollback_flags,
    master_param,
    first_moment,
    second_moment,
):
    shard_rows = master_param.shape[1]
    width = master_param.shape[2]
    gradient, squares = reduced(layer_inputs, key_cotangent, token_counts)
    total_sq = jnp.sum(squares[0])
    entries = lax.axis_size("section") * lax.axis_size("dp") * shard_rows * width
    clip_scale = clip_level * math.sqrt(entries) / (jnp.sqrt(total_sq) + 1e-06)
    clipped = gradient * clip_scale
    step_count = (1 + jnp.sum((rollback_flags == 0).astype(jnp.int32))).astype(jnp.float32)
    bias_one = 1.0 - jnp.power(jnp.float32(beta_first), step_count)
    bias_two = 1.0 - jnp.power(jnp.float32(beta_second), step_count)
    param_now = master_param[0]
    new_first = beta_first * first_moment[0] + (1.0 - beta_first) * clipped
    new_second = beta_second * second_moment[0] + (1.0 - beta_second) * clipped * clipped
    update_direction = (
        new_first / bias_one / (jnp.sqrt(new_second / bias_two) + adam_epsilon)
        + weight_decay * param_now
    )
    new_param = param_now - learn_rate * update_direction
    return (new_param[None], new_first[None], new_second[None], update_direction[None])


def solution(mesh):
    placed = (
        P("section", "dp", None),
        P("section", "dp", None),
        P("dp", None),
        P(),
        P("section", "dp", None),
        P("section", "dp", None),
        P("section", "dp", None),
    )
    return jax.shard_map(
        local,
        mesh=mesh,
        in_specs=placed,
        out_specs=(P("section", "dp", None),) * 4,
        check_vma=False,
    )
```

```python
import functools
import math

import jax
import jax.numpy as jnp
from jax import lax
from jax.experimental import pallas as pl
from jax.experimental.pallas import tpu as pltpu
from jax.sharding import PartitionSpec as P

beta_first = 0.9
beta_second = 0.95
adam_epsilon = 1e-08
weight_decay = 0.1
learn_rate = 0.00015
clip_level = 1.0

NX, NZ, NY = 4, 8, 4
MESH = pl.DeviceIdType.MESH
LIMIT = 32767.0
TINY = 1e-33

PIECES = {"A0": (0, 160), "B0": (160, 96), "A1": (256, 144), "B1": (400, 112)}
SIGN = {"A0": 1, "A1": -1, "B0": 1, "B1": -1}
STEP = {"A0": 160, "A1": 144, "B0": 96, "B1": 112}
DZ_ORDER = (4, 3, -3, 2, -2, 1, -1, 0)
DX_ORDER = (2, 1, -1, 0)

ORDER = (
    0, 96, 64, 32, 8, 104, 80, 41, 72, 84, 9, 112, 36, 124, 108, 88,
    68, 12, 120, 40, 17, 81, 49, 100, 16, 1, 76, 105, 97, 4, 65, 69,
    89, 60, 73, 34, 113, 109, 2, 77, 56, 85, 33, 101, 92, 42, 44, 24,
    116, 38, 10, 114, 5, 66, 52, 3, 98, 121, 6, 28, 125, 106, 82, 90,
    37, 102, 48, 45, 115, 35, 18, 110, 46, 117, 13, 11, 14, 99, 67, 26,
    7, 70, 83, 43, 50, 86, 20, 107, 39, 54, 122, 74, 25, 118, 103, 57,
    53, 19, 21, 78, 15, 58, 51, 71, 47, 22, 61, 75, 111, 93, 126, 87,
    62, 27, 91, 119, 123, 55, 30, 29, 59, 94, 79, 23, 127, 63, 31, 95,
)


def build_tasks():
    tasks = {}
    for c in ("A0", "A1"):
        sg = SIGN[c]
        for dz in DZ_ORDER:
            tasks[(c, "x", dz, 2 * sg)] = (c, (dz, 2), (), ("x", sg))
            tasks[(c, "x", dz, -sg)] = (c, (dz, -sg), (), ("x", -sg))
            tasks[(c, "x", dz, sg)] = (c, (dz, sg), ((c, "x", dz, 2 * sg),), ("x", sg))
            ins = [(c, "x", dz, sg), (c, "x", dz, -sg)]
            d = dz if dz != 4 else 4 * sg
            out = None
            if d == 0:
                ins += [(c, "z", sg), (c, "z", -sg)]
            else:
                s = 1 if d > 0 else -1
                if abs(d) < (4 if s == sg else 3):
                    ins.append((c, "z", d + s))
                out = ("z", s)
            tasks[(c, "z", d)] = (c, (dz, 0), tuple(ins), out)
    for c in ("B0", "B1"):
        sg = SIGN[c]
        for dx in DX_ORDER:
            for k in (4, 3, 2, 1):
                d = k * sg
                ins = () if k == 4 else ((c, "z", dx, d + sg),)
                tasks[(c, "z", dx, d)] = (c, (4 if k == 4 else d, dx), ins, ("z", sg))
            for k in (3, 2, 1):
                d = -k * sg
                ins = () if k == 3 else ((c, "z", dx, d - sg),)
                tasks[(c, "z", dx, d)] = (c, (d, dx), ins, ("z", -sg))
            ins = [(c, "z", dx, sg), (c, "z", dx, -sg)]
            out, d = None, dx
            if dx == 0:
                ins += [(c, "x", sg), (c, "x", -sg)]
            elif dx == 2:
                out, d = ("x", sg), 2 * sg
            elif dx == sg:
                ins.append((c, "x", 2 * sg))
                out = ("x", sg)
            else:
                out = ("x", -sg)
            tasks[(c, "x", d)] = (c, (0, dx), tuple(ins), out)
    return tasks


TASKS = build_tasks()
NAMES = list(TASKS)
SEQUENCE = [NAMES[i] for i in ORDER]
BLOCKS = list(dict.fromkeys(TASKS[n][1] for n in SEQUENCE))
MESSAGES = {}
for _n in SEQUENCE:
    if TASKS[_n][3] is not None:
        _c = TASKS[_n][0]
        MESSAGES[_n] = (_c, sum(1 for m in MESSAGES if MESSAGES[m][0] == _c))
N_MSG = 31
CLASSES = ("A0", "A1", "B0", "B1")
GROUP = 4
STEPS = 4


def kernel(entries, x_hbm, m_hbm, counts, flags, g_out, scale_out, xbuf, mbuf, masked, mt, part, tmp, grad, *rest):
    snd, rcv, hsnd, hrcv = rest[0:4], rest[4:8], rest[8:12], rest[12:16]
    ssem, rsem, hssem, hrsem, xsem, msem, red, redr0, redr1, s0, r0, s1, r1, turned, gsem, far, scale = rest[16:]
    width = mbuf.shape[1]
    section, dp = lax.axis_index("section"), lax.axis_index("dp")
    y, core = section // 2, lax.rem(section, 2)
    z, x = dp // NX, lax.rem(dp, NX)

    def at(dz=0, dx=0, dy=0, dc=0):
        return {
            "section": lax.rem(y + dy + NY, NY) * 2 + lax.rem(core + dc, 2),
            "dp": lax.rem(z + dz + NZ, NZ) * NX + lax.rem(x + dx + NX, NX),
        }

    plane = [(0, dx, dy, 0) for dx in range(NX) for dy in range(NY) if (dx, dy) != (0, 0)]
    column = [(dz, 0, 0, dc) for dz in range(NZ) for dc in range(2) if (dz, dc) != (0, 0)]

    mload = pltpu.make_async_copy(m_hbm.at[0], mbuf, msem)
    mload.start()

    def xload(i):
        dz, dx = BLOCKS[i]
        first = (lax.rem(z + dz + NZ, NZ) * NX + lax.rem(x + dx + NX, NX)) * 256
        return pltpu.make_async_copy(
            x_hbm.at[0, :, pl.ds(pl.multiple_of(first, 256), 256)], xbuf.at[i], xsem.at[i]
        )

    xload(0).start()

    barrier = pltpu.get_barrier_semaphore()
    peers = [(1, 0, 0, 0), (-1, 0, 0, 0), (0, 1, 0, 0), (0, -1, 0, 0)]
    peers += [(0, 0, 1, 0), (0, 0, -1, 0), (0, 0, 0, 1)]
    for peer in peers:
        pl.semaphore_signal(barrier, inc=1, device_id=at(*peer), device_id_type=MESH)

    mload.wait()
    for i in range(1, len(BLOCKS)):
        xload(i).start()
    per_micro = mbuf.shape[0] // counts.shape[1]
    for j in range(counts.shape[1]):
        rows = lax.broadcasted_iota(jnp.int32, (per_micro, width), 0)
        block = mbuf[j * per_micro : (j + 1) * per_micro, :].astype(jnp.float32)
        masked[j * per_micro : (j + 1) * per_micro, :] = jnp.where(rows < counts[0, j], block, 0.0)
    mt[...] = masked[...].T.astype(jnp.bfloat16)

    done = set()

    def need(block):
        if block in done:
            return
        i = BLOCKS.index(block)
        last = min(i + (GROUP if i >= GROUP else 1), len(BLOCKS))
        for j in range(i, last):
            done.add(BLOCKS[j])
            xload(j).wait()

        def dot(j, _):
            part[j] = jnp.dot(mt[...], xbuf[j], preferred_element_type=jnp.float32)
            return 0

        lax.fori_loop(i, last, dot, 0)

    def send(name):
        c, i = MESSAGES[name]
        axis, s = TASKS[name][3]
        k = CLASSES.index(c)
        to = at(dz=s) if axis == "z" else at(dx=s)
        return (
            pltpu.make_async_remote_copy(
                snd[k].at[i], rcv[k].at[i], ssem.at[k, i], rsem.at[k, i], device_id=to, device_id_type=MESH
            ),
            pltpu.make_async_remote_copy(
                hsnd[k].at[i], hrcv[k].at[i], hssem.at[k, i], hrsem.at[k, i], device_id=to, device_id_type=MESH
            ),
        )

    entered = False
    sums = jnp.zeros((8, 256), jnp.float32)
    for place, name in enumerate(SEQUENCE):
        c, block, ins, out = TASKS[name]
        if place == 24:
            pl.semaphore_wait(far, 1)
        first, rows = PIECES[c]
        k, step = CLASSES.index(c), STEP[c]
        need(block)
        b = BLOCKS.index(block)
        scales = []
        for n in ins:
            data, head = send(n)
            head.wait_recv()
            data.wait_recv()
            scales.append(hrcv[k][MESSAGES[n][1]])

        def value(r, size):
            acc = part[b, pl.ds(first + r, size), :]
            for n, scale in zip(ins, scales):
                acc = acc + rcv[k][MESSAGES[n][1], pl.ds(r, size), :].astype(jnp.float32) * scale
            return acc

        if out is None:

            def final(g, total):
                acc = value(g * step, step)
                grad[pl.ds(first + g * step, step), :] = acc
                return total + jnp.sum((acc * acc).reshape(step // 8, 8, 256), axis=0)

            sums = lax.fori_loop(0, rows // step, final, sums)
            continue

        def high(g, top):
            acc = value(g * step, step)
            if ins:
                tmp[pl.ds(g * step, step), :] = acc
            return jnp.maximum(top, jnp.max(jnp.abs(acc).reshape(step // 8, 8, 256), axis=0))

        top = lax.fori_loop(0, rows // step, high, jnp.full((8, 256), TINY, jnp.float32))
        top = jnp.max(top, axis=0, keepdims=True)
        i = MESSAGES[name][1]
        hsnd[k][i] = top * (1.0 / LIMIT)
        inverse = LIMIT / top

        def narrow(g, _):
            acc = tmp[pl.ds(g * step, step), :] if ins else part[b, pl.ds(first + g * step, step), :]
            snd[k][i, pl.ds(g * step, step), :] = jnp.round(acc * inverse).astype(jnp.int16)
            return 0

        lax.fori_loop(0, rows // step, narrow, 0)
        if not entered:
            pl.semaphore_wait(barrier, len(peers))
            pl.semaphore_signal(far, inc=1, device_id=at(0, 0, 1, 0), device_id_type=MESH)
            entered = True
        data, head = send(name)
        head.start()
        data.start()

    sums = jnp.sum(sums, axis=0, keepdims=True)
    red[0] = sums[:, :128] + sums[:, 128:]
    for q, (dirs, dst, ss, rs) in enumerate(((plane, redr0, s0, r0), (column, redr1, s1, r1))):
        for j, d in enumerate(dirs):
            pltpu.make_async_remote_copy(
                red.at[q], dst.at[j], ss, rs, device_id=at(*d), device_id_type=MESH
            ).start()
        if q == 0:
            for n in SEQUENCE:
                if TASKS[n][3] is not None:
                    data, head = send(n)
                    head.wait_send()
                    data.wait_send()
            for j in range(0, 256, 128):
                turned[j : j + 128, :] = grad[:, j : j + 128].T
            store = pltpu.make_async_copy(turned, g_out, gsem)
            store.start()
        whole = pltpu.make_async_remote_copy(dst, dst, ss, rs, device_id=at(*dirs[0]), device_id_type=MESH)
        whole.wait_recv()
        red[q + 1] = red[q] + jnp.sum(dst[...], axis=0)
        whole.wait_send()
    total_sq = jnp.sum(red[2], axis=1, keepdims=True)
    clip_scale = clip_level * math.sqrt(entries) / (jnp.sqrt(total_sq) + 1e-06)
    power_one, power_two = jnp.float32(beta_first), jnp.float32(beta_second)
    for i in range(flags.shape[0]):
        counted = flags[i] == 0
        power_one = power_one * jnp.where(counted, jnp.float32(beta_first), jnp.float32(1.0))
        power_two = power_two * jnp.where(counted, jnp.float32(beta_second), jnp.float32(1.0))
    shape = (1, width)
    scale[0:1, :] = jnp.broadcast_to(clip_scale, shape)
    scale[1:2, :] = 1.0 / (1.0 - jnp.full(shape, power_one, jnp.float32))
    scale[2:3, :] = 1.0 / (1.0 - jnp.full(shape, power_two, jnp.float32))
    scale[3:8, :] = jnp.zeros((5, width), jnp.float32)
    put = pltpu.make_async_copy(scale, scale_out, msem)
    put.start()
    put.wait()
    store.wait()


def reduced(layer_inputs, key_cotangent, token_counts, flags, entries):
    _, tokens, depth = layer_inputs.shape
    width = key_cotangent.shape[2]
    anywhere = pl.BlockSpec(memory_space=pltpu.HBM)
    pieces = [PIECES[c][1] for c in CLASSES]
    return pl.pallas_call(
        functools.partial(kernel, entries),
        out_shape=(
            jax.ShapeDtypeStruct((256, width), jnp.float32),
            jax.ShapeDtypeStruct((8, width), jnp.float32),
        ),
        in_specs=[anywhere, anywhere, *[pl.BlockSpec(memory_space=pltpu.SMEM)] * 2],
        out_specs=(anywhere, anywhere),
        scratch_shapes=[
            pltpu.VMEM((32, tokens, 256), jnp.bfloat16),
            pltpu.VMEM((tokens, width), jnp.bfloat16),
            pltpu.VMEM((tokens, width), jnp.float32),
            pltpu.VMEM((width, tokens), jnp.bfloat16),
            pltpu.VMEM((32, width, 256), jnp.float32),
            pltpu.VMEM((160, 256), jnp.float32),
            pltpu.VMEM((width, 256), jnp.float32),
            *[pltpu.VMEM((N_MSG, r, 256), jnp.int16) for r in pieces],
            *[pltpu.VMEM((N_MSG, r, 256), jnp.int16) for r in pieces],
            *[pltpu.VMEM((N_MSG, 1, 256), jnp.float32) for r in pieces],
            *[pltpu.VMEM((N_MSG, 1, 256), jnp.float32) for r in pieces],
            pltpu.SemaphoreType.DMA((4, N_MSG)),
            pltpu.SemaphoreType.DMA((4, N_MSG)),
            pltpu.SemaphoreType.DMA((4, N_MSG)),
            pltpu.SemaphoreType.DMA((4, N_MSG)),
            pltpu.SemaphoreType.DMA((32,)),
            pltpu.SemaphoreType.DMA,
            pltpu.VMEM((3, 1, 128), jnp.float32),
            pltpu.VMEM((15, 1, 128), jnp.float32),
            pltpu.VMEM((15, 1, 128), jnp.float32),
            pltpu.SemaphoreType.DMA,
            pltpu.SemaphoreType.DMA,
            pltpu.SemaphoreType.DMA,
            pltpu.SemaphoreType.DMA,
            pltpu.VMEM((256, width), jnp.float32),
            pltpu.SemaphoreType.DMA,
            pltpu.SemaphoreType.REGULAR,
            pltpu.VMEM((8, width), jnp.float32),
        ],
        compiler_params=pltpu.CompilerParams(
            collective_id=0, has_side_effects=True, vmem_limit_bytes=56 << 20
        ),
    )(layer_inputs, key_cotangent, token_counts, flags)


def update(grad, scale_hbm, param, first, second, *rest):
    outs, held, bufs, scale, gsem, sems, ssem = rest[:4], rest[4:8], rest[8:12], *rest[12:]
    step = bufs[0].shape[0] // STEPS
    get = pltpu.make_async_copy(scale_hbm, scale, ssem)
    get.start()
    loads = []
    for i in range(STEPS):
        part = pl.ds(i * step, step)
        sources = (grad.at[part], param.at[0, part], first.at[0, part], second.at[0, part])
        loads.append([])
        for j, source in enumerate(sources):
            loads[i].append(pltpu.make_async_copy(source, held[j].at[part], gsem.at[j, i]))
            loads[i][j].start()
    get.wait()
    unbias_one, unbias_two = scale[1:2, :], scale[2:3, :]
    stores = []
    for i in range(STEPS):
        part = pl.ds(i * step, step)
        for load in loads[i]:
            load.wait()
        clipped = held[0][part, :] * scale[0:1, :]
        now = held[1][part, :]
        one = beta_first * held[2][part, :] + (1.0 - beta_first) * clipped
        two = beta_second * held[3][part, :] + (1.0 - beta_second) * clipped * clipped
        turn = one * unbias_one / (jnp.sqrt(two * unbias_two) + adam_epsilon) + weight_decay * now
        for j, value in enumerate((now - learn_rate * turn, one, two, turn)):
            bufs[j][part, :] = value
            stores.append(pltpu.make_async_copy(bufs[j].at[part], outs[j].at[0, part], sems.at[j, i]))
            stores[-1].start()
    for store in stores:
        store.wait()


def local(
    layer_inputs,
    key_cotangent,
    token_counts,
    rollback_flags,
    master_param,
    first_moment,
    second_moment,
):
    _, shard_rows, width = master_param.shape
    entries = lax.axis_size("section") * lax.axis_size("dp") * shard_rows * width
    gradient, scale = reduced(layer_inputs, key_cotangent, token_counts, rollback_flags, entries)
    anywhere = pl.BlockSpec(memory_space=pltpu.HBM)
    return pl.pallas_call(
        update,
        out_shape=(jax.ShapeDtypeStruct(master_param.shape, jnp.float32),) * 4,
        in_specs=(anywhere,) * 5,
        out_specs=(anywhere,) * 4,
        scratch_shapes=[
            *[pltpu.VMEM((shard_rows, width), jnp.float32)] * 8,
            pltpu.VMEM((8, width), jnp.float32),
            pltpu.SemaphoreType.DMA((4, STEPS)),
            pltpu.SemaphoreType.DMA((4, STEPS)),
            pltpu.SemaphoreType.DMA,
        ],
        compiler_params=pltpu.CompilerParams(vmem_limit_bytes=60 << 20),
        cost_estimate=pl.CostEstimate(flops=20 << 17, bytes_accessed=4 << 20, transcendentals=1 << 17),
    )(gradient, scale, master_param, first_moment, second_moment)


def solution(mesh):
    placed = (
        P("section", "dp", None),
        P("section", "dp", None),
        P("dp", None),
        P(),
        P("section", "dp", None),
        P("section", "dp", None),
        P("section", "dp", None),
    )
    return jax.shard_map(
        local,
        mesh=mesh,
        in_specs=placed,
        out_specs=(P("section", "dp", None),) * 4,
        check_vma=False,
    )
```

```python
import functools
import math

import jax
import jax.numpy as jnp
from jax import lax
from jax.experimental import pallas as pl
from jax.experimental.pallas import tpu as pltpu
from jax.sharding import PartitionSpec as P

beta_first = 0.9
beta_second = 0.95
adam_epsilon = 1e-08
weight_decay = 0.1
learn_rate = 0.00015
clip_level = 1.0

NX, NZ, NY = 4, 8, 4
MESH = pl.DeviceIdType.MESH
LIMIT = 32767.0
TINY = 1e-33

PIECES = {"A0": (0, 160), "B0": (160, 96), "A1": (256, 144), "B1": (400, 112)}
SIGN = {"A0": 1, "A1": -1, "B0": 1, "B1": -1}
STEP = {"A0": 160, "A1": 144, "B0": 96, "B1": 112}
DZ_ORDER = (4, 3, -3, 2, -2, 1, -1, 0)
DX_ORDER = (2, 1, -1, 0)

ORDER = (
    0, 96, 64, 32, 8, 104, 80, 41, 72, 84, 9, 112, 36, 124, 108, 88,
    68, 12, 120, 40, 17, 81, 49, 100, 16, 1, 76, 105, 97, 4, 65, 69,
    89, 60, 73, 34, 113, 109, 2, 77, 56, 85, 33, 101, 92, 42, 44, 24,
    116, 38, 10, 114, 5, 66, 52, 3, 98, 121, 6, 28, 125, 106, 82, 90,
    37, 102, 48, 45, 115, 35, 18, 110, 46, 117, 13, 11, 14, 99, 67, 26,
    7, 70, 83, 43, 50, 86, 20, 107, 39, 54, 122, 74, 25, 118, 103, 57,
    53, 19, 21, 78, 15, 58, 51, 71, 47, 22, 61, 75, 111, 93, 126, 87,
    62, 27, 91, 119, 123, 55, 30, 29, 59, 94, 79, 23, 127, 63, 31, 95,
)


def build_tasks():
    tasks = {}
    for c in ("A0", "A1"):
        sg = SIGN[c]
        for dz in DZ_ORDER:
            tasks[(c, "x", dz, 2 * sg)] = (c, (dz, 2), (), ("x", sg))
            tasks[(c, "x", dz, -sg)] = (c, (dz, -sg), (), ("x", -sg))
            tasks[(c, "x", dz, sg)] = (c, (dz, sg), ((c, "x", dz, 2 * sg),), ("x", sg))
            ins = [(c, "x", dz, sg), (c, "x", dz, -sg)]
            d = dz if dz != 4 else 4 * sg
            out = None
            if d == 0:
                ins += [(c, "z", sg), (c, "z", -sg)]
            else:
                s = 1 if d > 0 else -1
                if abs(d) < (4 if s == sg else 3):
                    ins.append((c, "z", d + s))
                out = ("z", s)
            tasks[(c, "z", d)] = (c, (dz, 0), tuple(ins), out)
    for c in ("B0", "B1"):
        sg = SIGN[c]
        for dx in DX_ORDER:
            for k in (4, 3, 2, 1):
                d = k * sg
                ins = () if k == 4 else ((c, "z", dx, d + sg),)
                tasks[(c, "z", dx, d)] = (c, (4 if k == 4 else d, dx), ins, ("z", sg))
            for k in (3, 2, 1):
                d = -k * sg
                ins = () if k == 3 else ((c, "z", dx, d - sg),)
                tasks[(c, "z", dx, d)] = (c, (d, dx), ins, ("z", -sg))
            ins = [(c, "z", dx, sg), (c, "z", dx, -sg)]
            out, d = None, dx
            if dx == 0:
                ins += [(c, "x", sg), (c, "x", -sg)]
            elif dx == 2:
                out, d = ("x", sg), 2 * sg
            elif dx == sg:
                ins.append((c, "x", 2 * sg))
                out = ("x", sg)
            else:
                out = ("x", -sg)
            tasks[(c, "x", d)] = (c, (0, dx), tuple(ins), out)
    return tasks


TASKS = build_tasks()
NAMES = list(TASKS)
SEQUENCE = [NAMES[i] for i in ORDER]
BLOCKS = list(dict.fromkeys(TASKS[n][1] for n in SEQUENCE))
MESSAGES = {}
for _n in SEQUENCE:
    if TASKS[_n][3] is not None:
        _c = TASKS[_n][0]
        MESSAGES[_n] = (_c, sum(1 for m in MESSAGES if MESSAGES[m][0] == _c))
TAKERS = [n for n in SEQUENCE if TASKS[n][2]]
TAKER = {m: i for i, n in enumerate(TAKERS) for m in TASKS[n][2]}
N_MSG = 31
CLASSES = ("A0", "A1", "B0", "B1")
LANES = 128
GROUP = 4
STEPS = 4


def kernel(entries, x_hbm, m_hbm, counts_hbm, flags_hbm, g_out, scale_out, xbuf, mbuf, masked, mt, part, tmp, grad, *rest):
    snd, rcv, hsnd, hrcv = rest[0:4], rest[4:8], rest[8:12], rest[12:16]
    ssem, rsem, hssem, dummy, xsem, msem, red, redr0, redr1, s0, r0, s1, r1, turned, gsem, far, scale, counts, flags, csem, fsem = rest[16:]
    width = mbuf.shape[1]
    section, dp = lax.axis_index("section"), lax.axis_index("dp")
    y, core = section // 2, lax.rem(section, 2)
    z, x = dp // NX, lax.rem(dp, NX)

    def at(dz=0, dx=0, dy=0, dc=0):
        return {
            "section": lax.rem(y + dy + NY, NY) * 2 + lax.rem(core + dc, 2),
            "dp": lax.rem(z + dz + NZ, NZ) * NX + lax.rem(x + dx + NX, NX),
        }

    plane = [(0, dx, dy, 0) for dx in range(NX) for dy in range(NY) if (dx, dy) != (0, 0)]
    column = [(dz, 0, 0, dc) for dz in range(NZ) for dc in range(2) if (dz, dc) != (0, 0)]

    mload = pltpu.make_async_copy(m_hbm.at[0], mbuf, msem)
    mload.start()
    cload = pltpu.make_async_copy(counts_hbm, counts, csem)
    cload.start()

    def xload(i):
        dz, dx = BLOCKS[i]
        first = (lax.rem(z + dz + NZ, NZ) * NX + lax.rem(x + dx + NX, NX)) * 256
        return pltpu.make_async_copy(
            x_hbm.at[0, :, pl.ds(pl.multiple_of(first, 256), 256)], xbuf.at[i], xsem.at[0 if i == 0 else i // GROUP + 1]
        )

    xload(0).start()

    barrier = pltpu.get_barrier_semaphore()
    peers = [(1, 0, 0, 0), (-1, 0, 0, 0), (0, 1, 0, 0), (0, -1, 0, 0)]
    peers += [(0, 0, 1, 0), (0, 0, -1, 0), (0, 0, 0, 1)]
    for peer in peers:
        pl.semaphore_signal(barrier, inc=1, device_id=at(*peer), device_id_type=MESH)

    fload = pltpu.make_async_copy(flags_hbm, flags, fsem)
    fload.start()
    cload.wait()
    mload.wait()
    for i in range(1, len(BLOCKS)):
        xload(i).start()
    per_micro = mbuf.shape[0] // counts.shape[1]
    for j in range(counts.shape[1]):
        rows = lax.broadcasted_iota(jnp.int32, (per_micro, width), 0)
        block = mbuf[j * per_micro : (j + 1) * per_micro, :].astype(jnp.float32)
        masked[j * per_micro : (j + 1) * per_micro, :] = jnp.where(rows < counts[0, j], block, 0.0)
    mt[...] = masked[...].T.astype(jnp.bfloat16)

    done = set()

    def need(block):
        if block in done:
            return
        i = BLOCKS.index(block)
        last = 1 if i == 0 else (i // GROUP + 1) * GROUP
        done.update(BLOCKS[i:last])
        group = xbuf.at[pl.ds(i, last - i)]
        pltpu.make_async_copy(group, group, xsem.at[0 if i == 0 else i // GROUP + 1]).wait()

        def dot(j, _):
            part[j] = jnp.dot(mt[...], xbuf[j], preferred_element_type=jnp.float32)
            return 0

        lax.fori_loop(i, last, dot, 0)

    def send(name):
        c, i = MESSAGES[name]
        axis, s = TASKS[name][3]
        k = CLASSES.index(c)
        to = at(dz=s) if axis == "z" else at(dx=s)
        return (
            pltpu.make_async_remote_copy(
                snd[k].at[i], rcv[k].at[i], ssem.at[k], rsem.at[TAKER[name]], device_id=to, device_id_type=MESH
            ),
            pltpu.make_async_remote_copy(
                hsnd[k].at[i], hrcv[k].at[i], hssem.at[k], rsem.at[TAKER[name]], device_id=to, device_id_type=MESH
            ),
        )

    entered = False
    sums = jnp.zeros((8, 256), jnp.float32)
    for place, name in enumerate(SEQUENCE):
        c, block, ins, out = TASKS[name]
        if place == 24:
            pl.semaphore_wait(far, 1)
        first, rows = PIECES[c]
        k, step = CLASSES.index(c), STEP[c]
        need(block)
        b = BLOCKS.index(block)
        scales = []
        if ins:
            whole = dummy.at[pl.ds(0, len(ins) * (rows + 2))]
            pltpu.make_async_remote_copy(
                whole, whole, ssem.at[k], rsem.at[TAKER[ins[0]]], device_id=at(dx=1), device_id_type=MESH
            ).wait_recv()
        for n in ins:
            scales.append(hrcv[k][MESSAGES[n][1]])

        def value(r, size):
            acc = part[b, pl.ds(first + r, size), :]
            for n, scale in zip(ins, scales):
                acc = acc + rcv[k][MESSAGES[n][1], pl.ds(r, size), :].astype(jnp.float32) * scale
            return acc

        if out is None:

            def final(g, total):
                acc = value(g * step, step)
                grad[pl.ds(first + g * step, step), :] = acc
                return total + jnp.sum((acc * acc).reshape(step // 8, 8, 256), axis=0)

            sums = lax.fori_loop(0, rows // step, final, sums)
            continue

        def high(g, top):
            acc = value(g * step, step)
            if ins:
                tmp[pl.ds(g * step, step), :] = acc
            return jnp.maximum(top, jnp.max(jnp.abs(acc).reshape(step // 8, 8, 256), axis=0))

        top = lax.fori_loop(0, rows // step, high, jnp.full((8, 256), TINY, jnp.float32))
        top = jnp.max(top, axis=0, keepdims=True)
        i = MESSAGES[name][1]
        hsnd[k][i] = top * (1.0 / LIMIT)
        inverse = LIMIT / top

        def narrow(g, _):
            acc = tmp[pl.ds(g * step, step), :] if ins else part[b, pl.ds(first + g * step, step), :]
            snd[k][i, pl.ds(g * step, step), :] = jnp.round(acc * inverse).astype(jnp.int16)
            return 0

        lax.fori_loop(0, rows // step, narrow, 0)
        if not entered:
            pl.semaphore_wait(barrier, len(peers))
            pl.semaphore_signal(far, inc=1, device_id=at(0, 0, 1, 0), device_id_type=MESH)
            entered = True
        data, head = send(name)
        head.start()
        data.start()

    sums = jnp.sum(sums, axis=0, keepdims=True)
    red[0] = sums[:, :128] + sums[:, 128:]
    for q, (dirs, dst, ss, rs) in enumerate(((plane, redr0, s0, r0), (column, redr1, s1, r1))):
        for j, d in enumerate(dirs):
            pltpu.make_async_remote_copy(
                red.at[q], dst.at[j], ss, rs, device_id=at(*d), device_id_type=MESH
            ).start()
        if q == 0:
            for k in range(len(CLASSES)):
                for buf, sem in ((snd[k], ssem.at[k]), (hsnd[k], hssem.at[k])):
                    pltpu.make_async_remote_copy(
                        buf, buf, sem, rsem.at[0], device_id=at(dx=1), device_id_type=MESH
                    ).wait_send()
            for j in range(0, 256, 128):
                turned[j : j + 128, :] = grad[:, j : j + 128].T
            store = pltpu.make_async_copy(turned, g_out, gsem)
            store.start()
        whole = pltpu.make_async_remote_copy(dst, dst, ss, rs, device_id=at(*dirs[0]), device_id_type=MESH)
        whole.wait_recv()
        red[q + 1] = red[q] + jnp.sum(dst[...], axis=0)
        whole.wait_send()
    total_sq = jnp.sum(red[2], axis=1, keepdims=True)
    clip_scale = clip_level * math.sqrt(entries) / (jnp.sqrt(total_sq) + 1e-06)
    fload.wait()
    power_one, power_two = jnp.float32(beta_first), jnp.float32(beta_second)
    for i in range(flags.shape[0]):
        counted = flags[i] == 0
        power_one = power_one * jnp.where(counted, jnp.float32(beta_first), jnp.float32(1.0))
        power_two = power_two * jnp.where(counted, jnp.float32(beta_second), jnp.float32(1.0))
    shape = (1, width)
    scale[0:1, :] = jnp.broadcast_to(clip_scale, shape)
    scale[1:2, :] = 1.0 / (1.0 - jnp.full(shape, power_one, jnp.float32))
    scale[2:3, :] = 1.0 / (1.0 - jnp.full(shape, power_two, jnp.float32))
    scale[3:8, :] = jnp.zeros((5, width), jnp.float32)
    put = pltpu.make_async_copy(scale, scale_out, msem)
    put.start()
    put.wait()
    store.wait()


def reduced(layer_inputs, key_cotangent, token_counts, flags, entries):
    _, tokens, depth = layer_inputs.shape
    width = key_cotangent.shape[2]
    anywhere = pl.BlockSpec(memory_space=pltpu.HBM)
    pieces = [PIECES[c][1] for c in CLASSES]
    return pl.pallas_call(
        functools.partial(kernel, entries),
        out_shape=(
            jax.ShapeDtypeStruct((256, width), jnp.float32),
            jax.ShapeDtypeStruct((8, width), jnp.float32),
        ),
        in_specs=[anywhere] * 4,
        out_specs=(anywhere, anywhere),
        scratch_shapes=[
            pltpu.VMEM((32, tokens, 256), jnp.bfloat16),
            pltpu.VMEM((tokens, width), jnp.bfloat16),
            pltpu.VMEM((tokens, width), jnp.float32),
            pltpu.VMEM((width, tokens), jnp.bfloat16),
            pltpu.VMEM((32, width, 256), jnp.float32),
            pltpu.VMEM((160, 256), jnp.float32),
            pltpu.VMEM((width, 256), jnp.float32),
            *[pltpu.VMEM((N_MSG, r, 256), jnp.int16) for r in pieces],
            *[pltpu.VMEM((N_MSG, r, 256), jnp.int16) for r in pieces],
            *[pltpu.VMEM((N_MSG, 1, 256), jnp.float32) for r in pieces],
            *[pltpu.VMEM((N_MSG, 1, 256), jnp.float32) for r in pieces],
            pltpu.SemaphoreType.DMA((len(CLASSES),)),
            pltpu.SemaphoreType.DMA((len(TAKERS),)),
            pltpu.SemaphoreType.DMA((len(CLASSES),)),
            pltpu.VMEM((4 * 162, 1, LANES), jnp.float32),
            pltpu.SemaphoreType.DMA((len(BLOCKS) // GROUP + 1,)),
            pltpu.SemaphoreType.DMA,
            pltpu.VMEM((3, 1, 128), jnp.float32),
            pltpu.VMEM((15, 1, 128), jnp.float32),
            pltpu.VMEM((15, 1, 128), jnp.float32),
            pltpu.SemaphoreType.DMA,
            pltpu.SemaphoreType.DMA,
            pltpu.SemaphoreType.DMA,
            pltpu.SemaphoreType.DMA,
            pltpu.VMEM((256, width), jnp.float32),
            pltpu.SemaphoreType.DMA,
            pltpu.SemaphoreType.REGULAR,
            pltpu.VMEM((8, width), jnp.float32),
            pltpu.SMEM(token_counts.shape, jnp.int32),
            pltpu.SMEM(flags.shape, jnp.int32),
            pltpu.SemaphoreType.DMA,
            pltpu.SemaphoreType.DMA,
        ],
        compiler_params=pltpu.CompilerParams(
            collective_id=0, has_side_effects=True, vmem_limit_bytes=56 << 20
        ),
    )(layer_inputs, key_cotangent, token_counts, flags)


def update(grad, scale_hbm, param, first, second, *rest):
    outs, held, kept, scale, gsem, sems, ssem = rest[:4], *rest[4:]
    step = kept.shape[1] // STEPS
    get = pltpu.make_async_copy(scale_hbm, scale, ssem)
    get.start()
    parts = [pl.ds(i * step, step) for i in range(STEPS)]
    for i, part in enumerate(parts):
        sources = (grad.at[part], param.at[0, part], first.at[0, part], second.at[0, part])
        for j, source in enumerate(sources):
            pltpu.make_async_copy(source, held.at[j, part], gsem.at[i]).start()
    get.wait()
    unbias_one, unbias_two = scale[1:2, :], scale[2:3, :]
    for i, part in enumerate(parts):
        pltpu.make_async_copy(held.at[:, part], held.at[:, part], gsem.at[i]).wait()
        clipped = held[0, part, :] * scale[0:1, :]
        now = held[1, part, :]
        one = beta_first * held[2, part, :] + (1.0 - beta_first) * clipped
        two = beta_second * held[3, part, :] + (1.0 - beta_second) * clipped * clipped
        turn = one * unbias_one / (jnp.sqrt(two * unbias_two) + adam_epsilon) + weight_decay * now
        for j, value in enumerate((now - learn_rate * turn, one, two, turn)):
            kept[j, part, :] = value
            pltpu.make_async_copy(kept.at[j, part], outs[j].at[0, part], sems.at[j]).start()
    for j in range(4):
        pltpu.make_async_copy(kept.at[j], outs[j].at[0], sems.at[j]).wait()


def local(
    layer_inputs,
    key_cotangent,
    token_counts,
    rollback_flags,
    master_param,
    first_moment,
    second_moment,
):
    _, shard_rows, width = master_param.shape
    entries = lax.axis_size("section") * lax.axis_size("dp") * shard_rows * width
    gradient, scale = reduced(layer_inputs, key_cotangent, token_counts, rollback_flags, entries)
    anywhere = pl.BlockSpec(memory_space=pltpu.HBM)
    return pl.pallas_call(
        update,
        out_shape=(jax.ShapeDtypeStruct(master_param.shape, jnp.float32),) * 4,
        in_specs=(anywhere,) * 5,
        out_specs=(anywhere,) * 4,
        scratch_shapes=[
            pltpu.VMEM((4, shard_rows, width), jnp.float32),
            pltpu.VMEM((4, shard_rows, width), jnp.float32),
            pltpu.VMEM((8, width), jnp.float32),
            pltpu.SemaphoreType.DMA((STEPS,)),
            pltpu.SemaphoreType.DMA((4,)),
            pltpu.SemaphoreType.DMA,
        ],
        compiler_params=pltpu.CompilerParams(vmem_limit_bytes=60 << 20),
        cost_estimate=pl.CostEstimate(flops=20 << 17, bytes_accessed=4 << 20, transcendentals=1 << 17),
    )(gradient, scale, master_param, first_moment, second_moment)


def solution(mesh):
    placed = (
        P("section", "dp", None),
        P("section", "dp", None),
        P("dp", None),
        P(),
        P("section", "dp", None),
        P("section", "dp", None),
        P("section", "dp", None),
    )
    return jax.shard_map(
        local,
        mesh=mesh,
        in_specs=placed,
        out_specs=(P("section", "dp", None),) * 4,
        check_vma=False,
    )
```

```python
import functools
import math

import jax
import jax.numpy as jnp
from jax import lax
from jax.experimental import pallas as pl
from jax.experimental.pallas import tpu as pltpu
from jax.sharding import PartitionSpec as P

beta_first = 0.9
beta_second = 0.95
adam_epsilon = 1e-08
weight_decay = 0.1
learn_rate = 0.00015
clip_level = 1.0

NX, NZ, NY = 4, 8, 4
MESH = pl.DeviceIdType.MESH
LIMIT = 32767.0
TINY = 1e-33

PIECES = {"A0": (0, 160), "B0": (160, 96), "A1": (256, 144), "B1": (400, 112)}
SIGN = {"A0": 1, "A1": -1, "B0": 1, "B1": -1}
STEP = {"A0": 160, "A1": 144, "B0": 96, "B1": 112}
DZ_ORDER = (4, 3, -3, 2, -2, 1, -1, 0)
DX_ORDER = (2, 1, -1, 0)

ORDER = (
    0, 96, 64, 32, 8, 104, 80, 41, 72, 84, 9, 112, 36, 124, 108, 88,
    68, 12, 120, 40, 17, 81, 49, 100, 16, 1, 76, 105, 97, 4, 65, 69,
    89, 60, 73, 34, 113, 109, 2, 77, 56, 85, 33, 101, 92, 42, 44, 24,
    116, 38, 10, 114, 5, 66, 52, 3, 98, 121, 6, 28, 125, 106, 82, 90,
    37, 102, 48, 45, 115, 35, 18, 110, 46, 117, 13, 11, 14, 99, 67, 26,
    7, 70, 83, 43, 50, 86, 20, 107, 39, 54, 122, 74, 25, 118, 103, 57,
    53, 19, 21, 78, 15, 58, 51, 71, 47, 22, 61, 75, 111, 93, 126, 87,
    62, 27, 91, 119, 123, 55, 30, 29, 59, 94, 79, 23, 127, 63, 31, 95,
)


def build_tasks():
    tasks = {}
    for c in ("A0", "A1"):
        sg = SIGN[c]
        for dz in DZ_ORDER:
            tasks[(c, "x", dz, 2 * sg)] = (c, (dz, 2), (), ("x", sg))
            tasks[(c, "x", dz, -sg)] = (c, (dz, -sg), (), ("x", -sg))
            tasks[(c, "x", dz, sg)] = (c, (dz, sg), ((c, "x", dz, 2 * sg),), ("x", sg))
            ins = [(c, "x", dz, sg), (c, "x", dz, -sg)]
            d = dz if dz != 4 else 4 * sg
            out = None
            if d == 0:
                ins += [(c, "z", sg), (c, "z", -sg)]
            else:
                s = 1 if d > 0 else -1
                if abs(d) < (4 if s == sg else 3):
                    ins.append((c, "z", d + s))
                out = ("z", s)
            tasks[(c, "z", d)] = (c, (dz, 0), tuple(ins), out)
    for c in ("B0", "B1"):
        sg = SIGN[c]
        for dx in DX_ORDER:
            for k in (4, 3, 2, 1):
                d = k * sg
                ins = () if k == 4 else ((c, "z", dx, d + sg),)
                tasks[(c, "z", dx, d)] = (c, (4 if k == 4 else d, dx), ins, ("z", sg))
            for k in (3, 2, 1):
                d = -k * sg
                ins = () if k == 3 else ((c, "z", dx, d - sg),)
                tasks[(c, "z", dx, d)] = (c, (d, dx), ins, ("z", -sg))
            ins = [(c, "z", dx, sg), (c, "z", dx, -sg)]
            out, d = None, dx
            if dx == 0:
                ins += [(c, "x", sg), (c, "x", -sg)]
            elif dx == 2:
                out, d = ("x", sg), 2 * sg
            elif dx == sg:
                ins.append((c, "x", 2 * sg))
                out = ("x", sg)
            else:
                out = ("x", -sg)
            tasks[(c, "x", d)] = (c, (0, dx), tuple(ins), out)
    return tasks


TASKS = build_tasks()
NAMES = list(TASKS)
SEQUENCE = [NAMES[i] for i in ORDER]
BLOCKS = list(dict.fromkeys(TASKS[n][1] for n in SEQUENCE))
MESSAGES = {}
for _n in SEQUENCE:
    if TASKS[_n][3] is not None:
        _c = TASKS[_n][0]
        MESSAGES[_n] = (_c, sum(1 for m in MESSAGES if MESSAGES[m][0] == _c))
TAKERS = [n for n in SEQUENCE if TASKS[n][2]]
TAKER = {m: i for i, n in enumerate(TAKERS) for m in TASKS[n][2]}
N_MSG = 31
CLASSES = ("A0", "A1", "B0", "B1")
LANES = 128
GROUP = 4
STEPS = 4


def kernel(entries, x_hbm, m_hbm, counts_hbm, flags_hbm, g_out, scale_out, xbuf, mbuf, masked, mt, part, tmp, grad, *rest):
    snd, rcv, hsnd, hrcv = rest[0:4], rest[4:8], rest[8:12], rest[12:16]
    ssem, rsem, hssem, dummy, xsem, msem, red, heard, s0, r0, turned, gsem, far, scale, counts, flags, csem, fsem, kin = rest[16:]
    width = mbuf.shape[1]
    section, dp = lax.axis_index("section"), lax.axis_index("dp")
    y, core = section // 2, lax.rem(section, 2)
    z, x = dp // NX, lax.rem(dp, NX)

    def at(dz=0, dx=0, dy=0, dc=0):
        return {
            "section": lax.rem(y + dy + NY, NY) * 2 + lax.rem(core + dc, 2),
            "dp": lax.rem(z + dz + NZ, NZ) * NX + lax.rem(x + dx + NX, NX),
        }

    offsets = [
        (dz, dx, dy, dc) for dz in range(NZ) for dx in range(NX) for dy in range(NY) for dc in range(2)
    ]
    others = sorted(offsets[1:], key=lambda d: -sum(min(a, n - a) for a, n in zip(d, (NZ, NX, NY, 2))))

    barrier = pltpu.get_barrier_semaphore()
    peers = [(1, 0, 0, 0), (-1, 0, 0, 0), (0, 1, 0, 0), (0, -1, 0, 0)]
    peers += [(0, 0, 1, 0), (0, 0, -1, 0), (0, 0, 0, 1)]
    for peer in peers:
        pl.semaphore_signal(barrier, inc=1, device_id=at(*peer), device_id_type=MESH)

    mload = pltpu.make_async_copy(m_hbm.at[0], mbuf, msem)
    mload.start()
    cload = pltpu.make_async_copy(counts_hbm, counts, csem)
    cload.start()

    def xload(i):
        dz, dx = BLOCKS[i]
        first = (lax.rem(z + dz + NZ, NZ) * NX + lax.rem(x + dx + NX, NX)) * 256
        return pltpu.make_async_copy(
            x_hbm.at[0, :, pl.ds(pl.multiple_of(first, 256), 256)], xbuf.at[i], xsem.at[0 if i == 0 else i // GROUP + 1]
        )

    xload(0).start()

    fload = pltpu.make_async_copy(flags_hbm, flags, fsem)
    fload.start()
    cload.wait()
    mload.wait()
    for i in range(1, len(BLOCKS)):
        xload(i).start()
    per_micro = mbuf.shape[0] // counts.shape[1]
    for j in range(counts.shape[1]):
        rows = lax.broadcasted_iota(jnp.int32, (per_micro, width), 0)
        block = mbuf[j * per_micro : (j + 1) * per_micro, :].astype(jnp.float32)
        masked[j * per_micro : (j + 1) * per_micro, :] = jnp.where(rows < counts[0, j], block, 0.0)
    mt[...] = masked[...].T.astype(jnp.bfloat16)

    done = set()

    def need(block):
        if block in done:
            return
        i = BLOCKS.index(block)
        last = 1 if i == 0 else (i // GROUP + 1) * GROUP
        done.update(BLOCKS[i:last])
        group = xbuf.at[pl.ds(i, last - i)]
        pltpu.make_async_copy(group, group, xsem.at[0 if i == 0 else i // GROUP + 1]).wait()

        def dot(j, _):
            part[j] = jnp.dot(mt[...], xbuf[j], preferred_element_type=jnp.float32)
            return 0

        lax.fori_loop(i, last, dot, 0)

    def send(name):
        c, i = MESSAGES[name]
        axis, s = TASKS[name][3]
        k = CLASSES.index(c)
        to = at(dz=s) if axis == "z" else at(dx=s)
        return (
            pltpu.make_async_remote_copy(
                snd[k].at[i], rcv[k].at[i], ssem.at[k], rsem.at[TAKER[name]], device_id=to, device_id_type=MESH
            ),
            pltpu.make_async_remote_copy(
                hsnd[k].at[i], hrcv[k].at[i], hssem.at[k], rsem.at[TAKER[name]], device_id=to, device_id_type=MESH
            ),
        )

    entered = False
    sums = jnp.zeros((8, 256), jnp.float32)
    for place, name in enumerate(SEQUENCE):
        c, block, ins, out = TASKS[name]
        if place == 12:
            pl.semaphore_wait(far, 1)
            pl.semaphore_signal(kin, inc=1, device_id=at(0, 0, 0, 1), device_id_type=MESH)
        if place == 24:
            pl.semaphore_wait(kin, 1)
        first, rows = PIECES[c]
        k, step = CLASSES.index(c), STEP[c]
        need(block)
        b = BLOCKS.index(block)
        scales = []
        if ins:
            whole = dummy.at[pl.ds(0, len(ins) * (rows + 2))]
            pltpu.make_async_remote_copy(
                whole, whole, ssem.at[k], rsem.at[TAKER[ins[0]]], device_id=at(dx=1), device_id_type=MESH
            ).wait_recv()
        for n in ins:
            scales.append(hrcv[k][MESSAGES[n][1]])

        def value(r, size):
            acc = part[b, pl.ds(first + r, size), :]
            for n, scale in zip(ins, scales):
                acc = acc + rcv[k][MESSAGES[n][1], pl.ds(r, size), :].astype(jnp.float32) * scale
            return acc

        if out is None:

            def final(g, total):
                acc = value(g * step, step)
                grad[pl.ds(first + g * step, step), :] = acc
                return total + jnp.sum((acc * acc).reshape(step // 8, 8, 256), axis=0)

            sums = lax.fori_loop(0, rows // step, final, sums)
            continue

        def high(g, top):
            acc = value(g * step, step)
            if ins:
                tmp[pl.ds(g * step, step), :] = acc
            return jnp.maximum(top, jnp.max(jnp.abs(acc).reshape(step // 8, 8, 256), axis=0))

        top = lax.fori_loop(0, rows // step, high, jnp.full((8, 256), TINY, jnp.float32))
        top = jnp.max(top, axis=0, keepdims=True)
        i = MESSAGES[name][1]
        hsnd[k][i] = top * (1.0 / LIMIT)
        inverse = LIMIT / top

        def narrow(g, _):
            acc = tmp[pl.ds(g * step, step), :] if ins else part[b, pl.ds(first + g * step, step), :]
            snd[k][i, pl.ds(g * step, step), :] = jnp.round(acc * inverse).astype(jnp.int16)
            return 0

        lax.fori_loop(0, rows // step, narrow, 0)
        if not entered:
            pl.semaphore_wait(barrier, len(peers))
            pl.semaphore_signal(far, inc=1, device_id=at(0, 0, 1, 0), device_id_type=MESH)
            entered = True
        data, head = send(name)
        head.start()
        data.start()

    sums = jnp.sum(sums, axis=0, keepdims=True)
    red[...] = sums[:, :LANES] + sums[:, LANES:]
    zs = [lax.rem(z + d, NZ) * NX for d in range(NZ)]
    xs = [lax.rem(x + d, NX) for d in range(NX)]
    ys = [lax.rem(y + d, NY) * 2 for d in range(NY)]
    cs = [core, 1 - core]
    for j, (dz, dx, dy, dc) in enumerate(others):
        to = {"section": ys[dy] + cs[dc], "dp": zs[dz] + xs[dx]}
        pltpu.make_async_remote_copy(red, heard.at[j], s0, r0, device_id=to, device_id_type=MESH).start()
    for k in range(len(CLASSES)):
        for buf, sem in ((snd[k], ssem.at[k]), (hsnd[k], hssem.at[k])):
            pltpu.make_async_remote_copy(
                buf, buf, sem, rsem.at[0], device_id=at(dx=1), device_id_type=MESH
            ).wait_send()
    for j in range(0, 256, 128):
        turned[j : j + 128, :] = grad[:, j : j + 128].T
    store = pltpu.make_async_copy(turned, g_out, gsem)
    store.start()
    whole = pltpu.make_async_remote_copy(heard, heard, s0, r0, device_id=at(dx=1), device_id_type=MESH)
    whole.wait_recv()
    total_sq = jnp.sum(red[...] + jnp.sum(heard[...], axis=0), axis=1, keepdims=True)
    whole.wait_send()
    clip_scale = clip_level * math.sqrt(entries) / (jnp.sqrt(total_sq) + 1e-06)
    fload.wait()
    power_one, power_two = jnp.float32(beta_first), jnp.float32(beta_second)
    for i in range(flags.shape[0]):
        counted = flags[i] == 0
        power_one = power_one * jnp.where(counted, jnp.float32(beta_first), jnp.float32(1.0))
        power_two = power_two * jnp.where(counted, jnp.float32(beta_second), jnp.float32(1.0))
    shape = (1, width)
    scale[0:1, :] = jnp.broadcast_to(clip_scale, shape)
    scale[1:2, :] = 1.0 / (1.0 - jnp.full(shape, power_one, jnp.float32))
    scale[2:3, :] = 1.0 / (1.0 - jnp.full(shape, power_two, jnp.float32))
    scale[3:8, :] = jnp.zeros((5, width), jnp.float32)
    put = pltpu.make_async_copy(scale, scale_out, msem)
    put.start()
    put.wait()
    store.wait()


def reduced(layer_inputs, key_cotangent, token_counts, flags, entries):
    _, tokens, depth = layer_inputs.shape
    width = key_cotangent.shape[2]
    anywhere = pl.BlockSpec(memory_space=pltpu.HBM)
    pieces = [PIECES[c][1] for c in CLASSES]
    return pl.pallas_call(
        functools.partial(kernel, entries),
        out_shape=(
            jax.ShapeDtypeStruct((256, width), jnp.float32),
            jax.ShapeDtypeStruct((8, width), jnp.float32),
        ),
        in_specs=[anywhere] * 4,
        out_specs=(anywhere, anywhere),
        scratch_shapes=[
            pltpu.VMEM((32, tokens, 256), jnp.bfloat16),
            pltpu.VMEM((tokens, width), jnp.bfloat16),
            pltpu.VMEM((tokens, width), jnp.float32),
            pltpu.VMEM((width, tokens), jnp.bfloat16),
            pltpu.VMEM((32, width, 256), jnp.float32),
            pltpu.VMEM((160, 256), jnp.float32),
            pltpu.VMEM((width, 256), jnp.float32),
            *[pltpu.VMEM((N_MSG, r, 256), jnp.int16) for r in pieces],
            *[pltpu.VMEM((N_MSG, r, 256), jnp.int16) for r in pieces],
            *[pltpu.VMEM((N_MSG, 1, 256), jnp.float32) for r in pieces],
            *[pltpu.VMEM((N_MSG, 1, 256), jnp.float32) for r in pieces],
            pltpu.SemaphoreType.DMA((len(CLASSES),)),
            pltpu.SemaphoreType.DMA((len(TAKERS),)),
            pltpu.SemaphoreType.DMA((len(CLASSES),)),
            pltpu.VMEM((4 * 162, 1, LANES), jnp.float32),
            pltpu.SemaphoreType.DMA((len(BLOCKS) // GROUP + 1,)),
            pltpu.SemaphoreType.DMA,
            pltpu.VMEM((1, LANES), jnp.float32),
            pltpu.VMEM((255, 1, LANES), jnp.float32),
            pltpu.SemaphoreType.DMA,
            pltpu.SemaphoreType.DMA,
            pltpu.VMEM((256, width), jnp.float32),
            pltpu.SemaphoreType.DMA,
            pltpu.SemaphoreType.REGULAR,
            pltpu.VMEM((8, width), jnp.float32),
            pltpu.SMEM(token_counts.shape, jnp.int32),
            pltpu.SMEM(flags.shape, jnp.int32),
            pltpu.SemaphoreType.DMA,
            pltpu.SemaphoreType.DMA,
            pltpu.SemaphoreType.REGULAR,
        ],
        compiler_params=pltpu.CompilerParams(
            collective_id=0, has_side_effects=True, vmem_limit_bytes=56 << 20
        ),
    )(layer_inputs, key_cotangent, token_counts, flags)


def update(grad, scale_hbm, param, first, second, *rest):
    outs, held, kept, scale, gsem, sems, ssem = rest[:4], *rest[4:]
    step = kept.shape[1] // STEPS
    get = pltpu.make_async_copy(scale_hbm, scale, ssem)
    get.start()
    parts = [pl.ds(i * step, step) for i in range(STEPS)]
    for i, part in enumerate(parts):
        sources = (grad.at[part], param.at[0, part], first.at[0, part], second.at[0, part])
        for j, source in enumerate(sources):
            pltpu.make_async_copy(source, held.at[j, part], gsem.at[i]).start()
    get.wait()
    unbias_one, unbias_two = scale[1:2, :], scale[2:3, :]
    for i, part in enumerate(parts):
        pltpu.make_async_copy(held.at[:, part], held.at[:, part], gsem.at[i]).wait()
        clipped = held[0, part, :] * scale[0:1, :]
        now = held[1, part, :]
        one = beta_first * held[2, part, :] + (1.0 - beta_first) * clipped
        two = beta_second * held[3, part, :] + (1.0 - beta_second) * clipped * clipped
        turn = one * unbias_one / (jnp.sqrt(two * unbias_two) + adam_epsilon) + weight_decay * now
        for j, value in enumerate((now - learn_rate * turn, one, two, turn)):
            kept[j, part, :] = value
            pltpu.make_async_copy(kept.at[j, part], outs[j].at[0, part], sems.at[j]).start()
    for j in range(4):
        pltpu.make_async_copy(kept.at[j], outs[j].at[0], sems.at[j]).wait()


def local(
    layer_inputs,
    key_cotangent,
    token_counts,
    rollback_flags,
    master_param,
    first_moment,
    second_moment,
):
    _, shard_rows, width = master_param.shape
    entries = lax.axis_size("section") * lax.axis_size("dp") * shard_rows * width
    gradient, scale = reduced(layer_inputs, key_cotangent, token_counts, rollback_flags, entries)
    anywhere = pl.BlockSpec(memory_space=pltpu.HBM)
    return pl.pallas_call(
        update,
        out_shape=(jax.ShapeDtypeStruct(master_param.shape, jnp.float32),) * 4,
        in_specs=(anywhere,) * 5,
        out_specs=(anywhere,) * 4,
        scratch_shapes=[
            pltpu.VMEM((4, shard_rows, width), jnp.float32),
            pltpu.VMEM((4, shard_rows, width), jnp.float32),
            pltpu.VMEM((8, width), jnp.float32),
            pltpu.SemaphoreType.DMA((STEPS,)),
            pltpu.SemaphoreType.DMA((4,)),
            pltpu.SemaphoreType.DMA,
        ],
        compiler_params=pltpu.CompilerParams(vmem_limit_bytes=60 << 20),
        cost_estimate=pl.CostEstimate(flops=20 << 17, bytes_accessed=4 << 20, transcendentals=1 << 17),
    )(gradient, scale, master_param, first_moment, second_moment)


def solution(mesh):
    placed = (
        P("section", "dp", None),
        P("section", "dp", None),
        P("dp", None),
        P(),
        P("section", "dp", None),
        P("section", "dp", None),
        P("section", "dp", None),
    )
    return jax.shard_map(
        local,
        mesh=mesh,
        in_specs=placed,
        out_specs=(P("section", "dp", None),) * 4,
        check_vma=False,
    )
```

```python
import functools
import math

import jax
import jax.numpy as jnp
from jax import lax
from jax.experimental import pallas as pl
from jax.experimental.pallas import tpu as pltpu
from jax.sharding import PartitionSpec as P

beta_first = 0.9
beta_second = 0.95
adam_epsilon = 1e-08
weight_decay = 0.1
learn_rate = 0.00015
clip_level = 1.0

NX, NZ, NY = 4, 8, 4
MESH = pl.DeviceIdType.MESH
LIMIT = 32767.0
TINY = 1e-33

PIECES = {"A0": (0, 160), "B0": (160, 96), "A1": (256, 144), "B1": (400, 112)}
SIGN = {"A0": 1, "A1": -1, "B0": 1, "B1": -1}
STEP = {"A0": 160, "A1": 144, "B0": 96, "B1": 112}
DZ_ORDER = (4, 3, -3, 2, -2, 1, -1, 0)
DX_ORDER = (2, 1, -1, 0)
FLIP_Z, FLIP_X = (3, 2, 1), (1,)

ORDER = (
    96, 0, 32, 64, 80, 112, 4, 100, 36, 12, 44, 120, 116, 72, 40, 16,
    8, 104, 84, 76, 97, 108, 1, 2, 88, 81, 68, 65, 92, 9, 117, 73,
    34, 124, 33, 37, 101, 121, 13, 6, 48, 5, 98, 105, 38, 85, 113, 56,
    3, 45, 14, 41, 66, 109, 69, 93, 77, 10, 28, 35, 99, 46, 102, 106,
    82, 74, 7, 42, 67, 20, 18, 70, 24, 52, 114, 17, 89, 49, 39, 50,
    11, 125, 60, 21, 25, 110, 43, 107, 22, 58, 115, 122, 118, 103, 78, 15,
    19, 26, 86, 90, 47, 57, 83, 126, 54, 51, 71, 53, 75, 123, 61, 62,
    23, 29, 30, 27, 119, 91, 111, 94, 59, 55, 87, 79, 127, 31, 95, 63,
)


def build_tasks():
    tasks = {}
    for c in ("A0", "A1"):
        for dz in DZ_ORDER:
            sg = -SIGN[c] if dz in FLIP_Z else SIGN[c]
            tasks[(c, "x", dz, 2 * sg)] = (c, (dz, 2), (), ("x", sg))
            tasks[(c, "x", dz, -sg)] = (c, (dz, -sg), (), ("x", -sg))
            tasks[(c, "x", dz, sg)] = (c, (dz, sg), ((c, "x", dz, 2 * sg),), ("x", sg))
            ins = [(c, "x", dz, sg), (c, "x", dz, -sg)]
            sg = SIGN[c]
            d = dz if dz != 4 else 4 * sg
            out = None
            if d == 0:
                ins += [(c, "z", sg), (c, "z", -sg)]
            else:
                s = 1 if d > 0 else -1
                if abs(d) < (4 if s == sg else 3):
                    ins.append((c, "z", d + s))
                out = ("z", s)
            tasks[(c, "z", d)] = (c, (dz, 0), tuple(ins), out)
    for c in ("B0", "B1"):
        for dx in DX_ORDER:
            sg = -SIGN[c] if dx in FLIP_X else SIGN[c]
            for k in (4, 3, 2, 1):
                d = k * sg
                ins = () if k == 4 else ((c, "z", dx, d + sg),)
                tasks[(c, "z", dx, d)] = (c, (4 if k == 4 else d, dx), ins, ("z", sg))
            for k in (3, 2, 1):
                d = -k * sg
                ins = () if k == 3 else ((c, "z", dx, d - sg),)
                tasks[(c, "z", dx, d)] = (c, (d, dx), ins, ("z", -sg))
            ins = [(c, "z", dx, sg), (c, "z", dx, -sg)]
            sg = SIGN[c]
            out, d = None, dx
            if dx == 0:
                ins += [(c, "x", sg), (c, "x", -sg)]
            elif dx == 2:
                out, d = ("x", sg), 2 * sg
            elif dx == sg:
                ins.append((c, "x", 2 * sg))
                out = ("x", sg)
            else:
                out = ("x", -sg)
            tasks[(c, "x", d)] = (c, (0, dx), tuple(ins), out)
    return tasks


TASKS = build_tasks()
NAMES = list(TASKS)
SEQUENCE = [NAMES[i] for i in ORDER]
BLOCKS = list(dict.fromkeys(TASKS[n][1] for n in SEQUENCE))
MESSAGES = {}
for _n in SEQUENCE:
    if TASKS[_n][3] is not None:
        _c = TASKS[_n][0]
        MESSAGES[_n] = (_c, sum(1 for m in MESSAGES if MESSAGES[m][0] == _c))
TAKERS = [n for n in SEQUENCE if TASKS[n][2]]
TAKER = {m: i for i, n in enumerate(TAKERS) for m in TASKS[n][2]}
N_MSG = 31
CLASSES = ("A0", "A1", "B0", "B1")
LANES = 128
GROUP = 4
STEPS = 4


def kernel(x_hbm, m_hbm, counts_hbm, flags_hbm, g_out, scale_out, xbuf, mbuf, masked, mt, part, tmp, grad, *rest):
    snd, rcv, hsnd, hrcv = rest[0:4], rest[4:8], rest[8:12], rest[12:16]
    ssem, rsem, hssem, dummy, xsem, msem, red, heard, s0, r0, turned, gsem, far, scale, counts, flags, csem, fsem, kin = rest[16:]
    width = mbuf.shape[1]
    section, dp = lax.axis_index("section"), lax.axis_index("dp")
    y, core = section // 2, lax.rem(section, 2)
    z, x = dp // NX, lax.rem(dp, NX)

    def at(dz=0, dx=0, dy=0, dc=0):
        return {
            "section": lax.rem(y + dy + NY, NY) * 2 + lax.rem(core + dc, 2),
            "dp": lax.rem(z + dz + NZ, NZ) * NX + lax.rem(x + dx + NX, NX),
        }

    offsets = [
        (dz, dx, dy, dc) for dz in range(NZ) for dx in range(NX) for dy in range(NY) for dc in range(2)
    ]
    others = sorted(offsets[1:], key=lambda d: -sum(min(a, n - a) for a, n in zip(d, (NZ, NX, NY, 2))))

    barrier = pltpu.get_barrier_semaphore()
    peers = [(1, 0, 0, 0), (-1, 0, 0, 0), (0, 1, 0, 0), (0, -1, 0, 0)]
    peers += [(0, 0, 1, 0), (0, 0, -1, 0), (0, 0, 0, 1)]
    for peer in peers:
        pl.semaphore_signal(barrier, inc=1, device_id=at(*peer), device_id_type=MESH)

    mload = pltpu.make_async_copy(m_hbm.at[0], mbuf, msem)
    mload.start()
    cload = pltpu.make_async_copy(counts_hbm, counts, csem)
    cload.start()

    def xload(i):
        dz, dx = BLOCKS[i]
        first = (lax.rem(z + dz + NZ, NZ) * NX + lax.rem(x + dx + NX, NX)) * 256
        return pltpu.make_async_copy(
            x_hbm.at[0, :, pl.ds(pl.multiple_of(first, 256), 256)], xbuf.at[i], xsem.at[0 if i == 0 else i // GROUP + 1]
        )

    xload(0).start()

    fload = pltpu.make_async_copy(flags_hbm, flags, fsem)
    fload.start()
    cload.wait()
    mload.wait()
    for i in range(1, len(BLOCKS)):
        xload(i).start()
    per_micro = mbuf.shape[0] // counts.shape[1]
    for j in range(counts.shape[1]):
        rows = lax.broadcasted_iota(jnp.int32, (per_micro, width), 0)
        block = mbuf[j * per_micro : (j + 1) * per_micro, :].astype(jnp.float32)
        masked[j * per_micro : (j + 1) * per_micro, :] = jnp.where(rows < counts[0, j], block, 0.0)
    mt[...] = masked[...].T.astype(jnp.bfloat16)

    done = set()

    def need(block):
        if block in done:
            return
        i = BLOCKS.index(block)
        last = 1 if i == 0 else (i // GROUP + 1) * GROUP
        done.update(BLOCKS[i:last])
        group = xbuf.at[pl.ds(i, last - i)]
        pltpu.make_async_copy(group, group, xsem.at[0 if i == 0 else i // GROUP + 1]).wait()

        def dot(j, _):
            part[j] = jnp.dot(mt[...], xbuf[j], preferred_element_type=jnp.float32)
            return 0

        lax.fori_loop(i, last, dot, 0)

    def send(name):
        c, i = MESSAGES[name]
        axis, s = TASKS[name][3]
        k = CLASSES.index(c)
        to = at(dz=s) if axis == "z" else at(dx=s)
        return (
            pltpu.make_async_remote_copy(
                snd[k].at[i], rcv[k].at[i], ssem.at[k], rsem.at[TAKER[name]], device_id=to, device_id_type=MESH
            ),
            pltpu.make_async_remote_copy(
                hsnd[k].at[i], hrcv[k].at[i], hssem.at[k], rsem.at[TAKER[name]], device_id=to, device_id_type=MESH
            ),
        )

    entered = False
    sums = jnp.zeros((8, 256), jnp.float32)
    for place, name in enumerate(SEQUENCE):
        c, block, ins, out = TASKS[name]
        if place == 10:
            pl.semaphore_wait(far, 1)
            pl.semaphore_signal(kin, inc=1, device_id=at(0, 0, 0, 1), device_id_type=MESH)
        if place == 20:
            pl.semaphore_wait(kin, 1)
        first, rows = PIECES[c]
        k, step = CLASSES.index(c), STEP[c]
        need(block)
        b = BLOCKS.index(block)
        scales = []
        if ins:
            whole = dummy.at[pl.ds(0, len(ins) * (rows + 1))]
            pltpu.make_async_remote_copy(
                whole, whole, ssem.at[k], rsem.at[TAKER[ins[0]]], device_id=at(dx=1), device_id_type=MESH
            ).wait_recv()
        for n in ins:
            scales.append(jnp.concatenate([hrcv[k][MESSAGES[n][1]]] * 2, axis=1))

        def value(r, size):
            acc = part[b, pl.ds(first + r, size), :]
            for n, scale in zip(ins, scales):
                acc = acc + rcv[k][MESSAGES[n][1], pl.ds(r, size), :].astype(jnp.float32) * scale
            return acc

        if out is None:

            def final(g, total):
                acc = value(g * step, step)
                grad[pl.ds(first + g * step, step), :] = acc
                return total + jnp.sum((acc * acc).reshape(step // 8, 8, 256), axis=0)

            sums = lax.fori_loop(0, rows // step, final, sums)
            continue

        def high(g, top):
            acc = value(g * step, step)
            if ins:
                tmp[pl.ds(g * step, step), :] = acc
            return jnp.maximum(top, jnp.max(jnp.abs(acc).reshape(step // 8, 8, 256), axis=0))

        top = lax.fori_loop(0, rows // step, high, jnp.full((8, 256), TINY, jnp.float32))
        top = jnp.max(jnp.maximum(top[:, :LANES], top[:, LANES:]), axis=0, keepdims=True)
        i = MESSAGES[name][1]
        hsnd[k][i] = top * (1.0 / LIMIT)
        inverse = jnp.concatenate([LIMIT / top] * 2, axis=1)

        def narrow(g, _):
            acc = tmp[pl.ds(g * step, step), :] if ins else part[b, pl.ds(first + g * step, step), :]
            snd[k][i, pl.ds(g * step, step), :] = jnp.round(acc * inverse).astype(jnp.int16)
            return 0

        lax.fori_loop(0, rows // step, narrow, 0)
        if not entered:
            pl.semaphore_wait(barrier, len(peers))
            pl.semaphore_signal(far, inc=1, device_id=at(0, 0, 1, 0), device_id_type=MESH)
            entered = True
        data, head = send(name)
        head.start()
        data.start()

    sums = jnp.sum(sums, axis=0, keepdims=True)
    red[...] = sums[:, :LANES] + sums[:, LANES:]
    zs = [lax.rem(z + d, NZ) * NX for d in range(NZ)]
    xs = [lax.rem(x + d, NX) for d in range(NX)]
    ys = [lax.rem(y + d, NY) * 2 for d in range(NY)]
    cs = [core, 1 - core]
    for j, (dz, dx, dy, dc) in enumerate(others):
        to = {"section": ys[dy] + cs[dc], "dp": zs[dz] + xs[dx]}
        pltpu.make_async_remote_copy(red, heard.at[j], s0, r0, device_id=to, device_id_type=MESH).start()
    for k in range(len(CLASSES)):
        for buf, sem in ((snd[k], ssem.at[k]), (hsnd[k], hssem.at[k])):
            pltpu.make_async_remote_copy(
                buf, buf, sem, rsem.at[0], device_id=at(dx=1), device_id_type=MESH
            ).wait_send()
    for j in range(0, 256, 128):
        turned[j : j + 128, :] = grad[:, j : j + 128].T
    store = pltpu.make_async_copy(turned, g_out, gsem)
    store.start()
    whole = pltpu.make_async_remote_copy(heard, heard, s0, r0, device_id=at(dx=1), device_id_type=MESH)
    fload.wait()
    power_one, power_two = jnp.float32(beta_first), jnp.float32(beta_second)
    for i in range(flags.shape[0]):
        counted = flags[i] == 0
        power_one = power_one * jnp.where(counted, jnp.float32(beta_first), jnp.float32(1.0))
        power_two = power_two * jnp.where(counted, jnp.float32(beta_second), jnp.float32(1.0))
    shape = (1, width)
    scale[1:2, :] = 1.0 / (1.0 - jnp.full(shape, power_one, jnp.float32))
    scale[2:3, :] = 1.0 / (1.0 - jnp.full(shape, power_two, jnp.float32))
    scale[3:8, :] = jnp.zeros((5, width), jnp.float32)
    scale[0:1, LANES:] = jnp.zeros((1, width - LANES), jnp.float32)
    whole.wait_recv()
    scale[0:1, :LANES] = red[...] + jnp.sum(heard[...], axis=0)
    put = pltpu.make_async_copy(scale, scale_out, msem)
    put.start()
    whole.wait_send()
    put.wait()
    store.wait()


def reduced(layer_inputs, key_cotangent, token_counts, flags):
    _, tokens, depth = layer_inputs.shape
    width = key_cotangent.shape[2]
    anywhere = pl.BlockSpec(memory_space=pltpu.HBM)
    pieces = [PIECES[c][1] for c in CLASSES]
    return pl.pallas_call(
        kernel,
        out_shape=(
            jax.ShapeDtypeStruct((256, width), jnp.float32),
            jax.ShapeDtypeStruct((8, width), jnp.float32),
        ),
        in_specs=[anywhere] * 4,
        out_specs=(anywhere, anywhere),
        scratch_shapes=[
            pltpu.VMEM((32, tokens, 256), jnp.bfloat16),
            pltpu.VMEM((tokens, width), jnp.bfloat16),
            pltpu.VMEM((tokens, width), jnp.float32),
            pltpu.VMEM((width, tokens), jnp.bfloat16),
            pltpu.VMEM((32, width, 256), jnp.float32),
            pltpu.VMEM((160, 256), jnp.float32),
            pltpu.VMEM((width, 256), jnp.float32),
            *[pltpu.VMEM((N_MSG, r, 256), jnp.int16) for r in pieces],
            *[pltpu.VMEM((N_MSG, r, 256), jnp.int16) for r in pieces],
            *[pltpu.VMEM((N_MSG, 1, LANES), jnp.float32) for r in pieces],
            *[pltpu.VMEM((N_MSG, 1, LANES), jnp.float32) for r in pieces],
            pltpu.SemaphoreType.DMA((len(CLASSES),)),
            pltpu.SemaphoreType.DMA((len(TAKERS),)),
            pltpu.SemaphoreType.DMA((len(CLASSES),)),
            pltpu.VMEM((4 * 161, 1, LANES), jnp.float32),
            pltpu.SemaphoreType.DMA((len(BLOCKS) // GROUP + 1,)),
            pltpu.SemaphoreType.DMA,
            pltpu.VMEM((1, LANES), jnp.float32),
            pltpu.VMEM((255, 1, LANES), jnp.float32),
            pltpu.SemaphoreType.DMA,
            pltpu.SemaphoreType.DMA,
            pltpu.VMEM((256, width), jnp.float32),
            pltpu.SemaphoreType.DMA,
            pltpu.SemaphoreType.REGULAR,
            pltpu.VMEM((8, width), jnp.float32),
            pltpu.SMEM(token_counts.shape, jnp.int32),
            pltpu.SMEM(flags.shape, jnp.int32),
            pltpu.SemaphoreType.DMA,
            pltpu.SemaphoreType.DMA,
            pltpu.SemaphoreType.REGULAR,
        ],
        compiler_params=pltpu.CompilerParams(
            collective_id=0, has_side_effects=True, vmem_limit_bytes=56 << 20
        ),
    )(layer_inputs, key_cotangent, token_counts, flags)


def update(entries, grad, scale_hbm, param, first, second, *rest):
    outs, held, kept, scale, gsem, sems, ssem = rest[:4], *rest[4:]
    step = kept.shape[1] // STEPS
    get = pltpu.make_async_copy(scale_hbm, scale, ssem)
    get.start()
    parts = [pl.ds(i * step, step) for i in range(STEPS)]
    for i, part in enumerate(parts):
        sources = (grad.at[part], param.at[0, part], first.at[0, part], second.at[0, part])
        for j, source in enumerate(sources):
            pltpu.make_async_copy(source, held.at[j, part], gsem.at[i]).start()
    get.wait()
    unbias_one, unbias_two = scale[1:2, :], scale[2:3, :]
    total_sq = jnp.sum(scale[0:1, :], axis=1, keepdims=True)
    clip_scale = clip_level * math.sqrt(entries) / (jnp.sqrt(total_sq) + 1e-06)
    clip_scale = jnp.broadcast_to(clip_scale, unbias_one.shape)
    for i, part in enumerate(parts):
        pltpu.make_async_copy(held.at[:, part], held.at[:, part], gsem.at[i]).wait()
        clipped = held[0, part, :] * clip_scale
        now = held[1, part, :]
        one = beta_first * held[2, part, :] + (1.0 - beta_first) * clipped
        two = beta_second * held[3, part, :] + (1.0 - beta_second) * clipped * clipped
        turn = one * unbias_one / (jnp.sqrt(two * unbias_two) + adam_epsilon) + weight_decay * now
        for j, value in enumerate((now - learn_rate * turn, one, two, turn)):
            kept[j, part, :] = value
            pltpu.make_async_copy(kept.at[j, part], outs[j].at[0, part], sems.at[j]).start()
    for j in range(4):
        pltpu.make_async_copy(kept.at[j], outs[j].at[0], sems.at[j]).wait()


def local(
    layer_inputs,
    key_cotangent,
    token_counts,
    rollback_flags,
    master_param,
    first_moment,
    second_moment,
):
    _, shard_rows, width = master_param.shape
    entries = lax.axis_size("section") * lax.axis_size("dp") * shard_rows * width
    gradient, scale = reduced(layer_inputs, key_cotangent, token_counts, rollback_flags)
    anywhere = pl.BlockSpec(memory_space=pltpu.HBM)
    return pl.pallas_call(
        functools.partial(update, entries),
        out_shape=(jax.ShapeDtypeStruct(master_param.shape, jnp.float32),) * 4,
        in_specs=(anywhere,) * 5,
        out_specs=(anywhere,) * 4,
        scratch_shapes=[
            pltpu.VMEM((4, shard_rows, width), jnp.float32),
            pltpu.VMEM((4, shard_rows, width), jnp.float32),
            pltpu.VMEM((8, width), jnp.float32),
            pltpu.SemaphoreType.DMA((STEPS,)),
            pltpu.SemaphoreType.DMA((4,)),
            pltpu.SemaphoreType.DMA,
        ],
        compiler_params=pltpu.CompilerParams(vmem_limit_bytes=60 << 20),
        cost_estimate=pl.CostEstimate(flops=20 << 17, bytes_accessed=4 << 20, transcendentals=1 << 17),
    )(gradient, scale, master_param, first_moment, second_moment)


def solution(mesh):
    placed = (
        P("section", "dp", None),
        P("section", "dp", None),
        P("dp", None),
        P(),
        P("section", "dp", None),
        P("section", "dp", None),
        P("section", "dp", None),
    )
    return jax.shard_map(
        local,
        mesh=mesh,
        in_specs=placed,
        out_specs=(P("section", "dp", None),) * 4,
        check_vma=False,
    )
```

```python
import functools
import math

import jax
import jax.numpy as jnp
from jax import lax
from jax.experimental import pallas as pl
from jax.experimental.pallas import tpu as pltpu
from jax.sharding import PartitionSpec as P

beta_first = 0.9
beta_second = 0.95
adam_epsilon = 1e-08
weight_decay = 0.1
learn_rate = 0.00015
clip_level = 1.0

NX, NZ, NY = 4, 8, 4
MESH = pl.DeviceIdType.MESH
LIMIT = 32767.0
TINY = 1e-33

PIECES = {"A0": (0, 160), "B0": (160, 96), "A1": (256, 144), "B1": (400, 112)}
SIGN = {"A0": 1, "A1": -1, "B0": 1, "B1": -1}
STEP = {"A0": 160, "A1": 144, "B0": 96, "B1": 112}
DZ_ORDER = (4, 3, -3, 2, -2, 1, -1, 0)
DX_ORDER = (2, 1, -1, 0)
FLIP_Z, FLIP_X = (3, 2, 1), (1,)

ORDER = (
    96, 0, 32, 64, 80, 112, 4, 100, 36, 12, 44, 120, 116, 72, 40, 16,
    8, 104, 84, 76, 97, 108, 1, 2, 88, 81, 68, 65, 92, 9, 117, 73,
    34, 124, 33, 37, 101, 121, 13, 6, 48, 5, 98, 105, 38, 85, 113, 56,
    3, 45, 14, 41, 66, 109, 69, 93, 77, 10, 28, 35, 99, 46, 102, 106,
    82, 74, 7, 42, 67, 20, 18, 70, 24, 52, 114, 17, 89, 49, 39, 50,
    11, 125, 60, 21, 25, 110, 43, 107, 22, 58, 115, 122, 118, 103, 78, 15,
    19, 26, 86, 90, 47, 57, 83, 126, 54, 51, 71, 53, 75, 123, 61, 62,
    23, 29, 30, 27, 119, 91, 111, 94, 59, 55, 87, 79, 127, 31, 95, 63,
)


def build_tasks():
    tasks = {}
    for c in ("A0", "A1"):
        for dz in DZ_ORDER:
            sg = -SIGN[c] if dz in FLIP_Z else SIGN[c]
            tasks[(c, "x", dz, 2 * sg)] = (c, (dz, 2), (), ("x", sg))
            tasks[(c, "x", dz, -sg)] = (c, (dz, -sg), (), ("x", -sg))
            tasks[(c, "x", dz, sg)] = (c, (dz, sg), ((c, "x", dz, 2 * sg),), ("x", sg))
            ins = [(c, "x", dz, sg), (c, "x", dz, -sg)]
            sg = SIGN[c]
            d = dz if dz != 4 else 4 * sg
            out = None
            if d == 0:
                ins += [(c, "z", sg), (c, "z", -sg)]
            else:
                s = 1 if d > 0 else -1
                if abs(d) < (4 if s == sg else 3):
                    ins.append((c, "z", d + s))
                out = ("z", s)
            tasks[(c, "z", d)] = (c, (dz, 0), tuple(ins), out)
    for c in ("B0", "B1"):
        for dx in DX_ORDER:
            sg = -SIGN[c] if dx in FLIP_X else SIGN[c]
            for k in (4, 3, 2, 1):
                d = k * sg
                ins = () if k == 4 else ((c, "z", dx, d + sg),)
                tasks[(c, "z", dx, d)] = (c, (4 if k == 4 else d, dx), ins, ("z", sg))
            for k in (3, 2, 1):
                d = -k * sg
                ins = () if k == 3 else ((c, "z", dx, d - sg),)
                tasks[(c, "z", dx, d)] = (c, (d, dx), ins, ("z", -sg))
            ins = [(c, "z", dx, sg), (c, "z", dx, -sg)]
            sg = SIGN[c]
            out, d = None, dx
            if dx == 0:
                ins += [(c, "x", sg), (c, "x", -sg)]
            elif dx == 2:
                out, d = ("x", sg), 2 * sg
            elif dx == sg:
                ins.append((c, "x", 2 * sg))
                out = ("x", sg)
            else:
                out = ("x", -sg)
            tasks[(c, "x", d)] = (c, (0, dx), tuple(ins), out)
    return tasks


TASKS = build_tasks()
NAMES = list(TASKS)
SEQUENCE = [NAMES[i] for i in ORDER]
BLOCKS = list(dict.fromkeys(TASKS[n][1] for n in SEQUENCE))
MESSAGES = {}
for _n in SEQUENCE:
    if TASKS[_n][3] is not None:
        _c = TASKS[_n][0]
        MESSAGES[_n] = (_c, sum(1 for m in MESSAGES if MESSAGES[m][0] == _c))
TAKERS = [n for n in SEQUENCE if TASKS[n][2]]
SLOT = (
    0, 1, 2, 3, 4, 5, 6, 7, 8, 9, 10, 11, 12, 13, 14, 15, 16, 17, 18, 19,
    20, 21, 22, 23, 24, 25, 26, 0, 27, 28, 29, 30, 31, 32, 1, 33, 34, 35, 36, 37,
    38, 2, 39, 3, 4, 40, 5, 41, 42, 43, 44, 45, 6, 7, 46, 8, 47, 9, 10, 48,
    49, 50, 11, 0, 12, 51, 52, 13, 14, 1, 15, 53, 16, 17, 18, 19, 20, 21, 2, 22,
)
TAKER = {m: SLOT[i] for i, n in enumerate(TAKERS) for m in TASKS[n][2]}
N_MSG = 31
CLASSES = ("A0", "A1", "B0", "B1")
LANES = 128
GROUP = 4
STEPS = 4


def kernel(x_hbm, m_hbm, counts_hbm, flags_hbm, g_out, scale_out, xbuf, mbuf, masked, mt, part, tmp, grad, *rest):
    snd, rcv, hsnd, hrcv = rest[0:4], rest[4:8], rest[8:12], rest[12:16]
    ssem, rsem, hssem, dummy, xsem, msem, red, heard, s0, r0, turned, gsem, far, scale, counts, flags, csem, fsem, kin = rest[16:]
    width = mbuf.shape[1]
    section, dp = lax.axis_index("section"), lax.axis_index("dp")
    y, core = section // 2, lax.rem(section, 2)
    z, x = dp // NX, lax.rem(dp, NX)

    def at(dz=0, dx=0, dy=0, dc=0):
        return {
            "section": lax.rem(y + dy + NY, NY) * 2 + lax.rem(core + dc, 2),
            "dp": lax.rem(z + dz + NZ, NZ) * NX + lax.rem(x + dx + NX, NX),
        }

    offsets = [
        (dz, dx, dy, dc) for dz in range(NZ) for dx in range(NX) for dy in range(NY) for dc in range(2)
    ]
    others = sorted(offsets[1:], key=lambda d: -sum(min(a, n - a) for a, n in zip(d, (NZ, NX, NY, 2))))

    barrier = pltpu.get_barrier_semaphore()
    peers = [(1, 0, 0, 0), (-1, 0, 0, 0), (0, 1, 0, 0), (0, -1, 0, 0)]
    peers += [(0, 0, 1, 0), (0, 0, -1, 0), (0, 0, 0, 1)]
    for peer in peers:
        pl.semaphore_signal(barrier, inc=1, device_id=at(*peer), device_id_type=MESH)

    mload = pltpu.make_async_copy(m_hbm.at[0], mbuf, msem)
    mload.start()
    cload = pltpu.make_async_copy(counts_hbm, counts, csem)
    cload.start()

    def xload(i):
        dz, dx = BLOCKS[i]
        first = (lax.rem(z + dz + NZ, NZ) * NX + lax.rem(x + dx + NX, NX)) * 256
        return pltpu.make_async_copy(
            x_hbm.at[0, :, pl.ds(pl.multiple_of(first, 256), 256)], xbuf.at[i], xsem.at[0 if i == 0 else i // GROUP + 1]
        )

    xload(0).start()

    fload = pltpu.make_async_copy(flags_hbm, flags, fsem)
    fload.start()
    cload.wait()
    mload.wait()
    for i in range(1, len(BLOCKS)):
        xload(i).start()
    per_micro = mbuf.shape[0] // counts.shape[1]
    for j in range(counts.shape[1]):
        rows = lax.broadcasted_iota(jnp.int32, (per_micro, width), 0)
        block = mbuf[j * per_micro : (j + 1) * per_micro, :].astype(jnp.float32)
        masked[j * per_micro : (j + 1) * per_micro, :] = jnp.where(rows < counts[0, j], block, 0.0)
    mt[...] = masked[...].T.astype(jnp.bfloat16)

    done = set()

    def need(block):
        if block in done:
            return
        i = BLOCKS.index(block)
        last = 1 if i == 0 else (i // GROUP + 1) * GROUP
        done.update(BLOCKS[i:last])
        group = xbuf.at[pl.ds(i, last - i)]
        pltpu.make_async_copy(group, group, xsem.at[0 if i == 0 else i // GROUP + 1]).wait()

        def dot(j, _):
            part[j] = jnp.dot(mt[...], xbuf[j], preferred_element_type=jnp.float32)
            return 0

        lax.fori_loop(i, last, dot, 0)

    def send(name):
        c, i = MESSAGES[name]
        axis, s = TASKS[name][3]
        k = CLASSES.index(c)
        to = at(dz=s) if axis == "z" else at(dx=s)
        return (
            pltpu.make_async_remote_copy(
                snd[k].at[i], rcv[k].at[i], ssem.at[k], rsem.at[TAKER[name]], device_id=to, device_id_type=MESH
            ),
            pltpu.make_async_remote_copy(
                hsnd[k].at[i], hrcv[k].at[i], hssem.at[k], rsem.at[TAKER[name]], device_id=to, device_id_type=MESH
            ),
        )

    entered = False
    sums = jnp.zeros((8, 256), jnp.float32)
    for place, name in enumerate(SEQUENCE):
        c, block, ins, out = TASKS[name]
        if place == 10:
            pl.semaphore_wait(far, 1)
            pl.semaphore_signal(kin, inc=1, device_id=at(0, 0, 0, 1), device_id_type=MESH)
        if place == 20:
            pl.semaphore_wait(kin, 1)
        first, rows = PIECES[c]
        k, step = CLASSES.index(c), STEP[c]
        need(block)
        b = BLOCKS.index(block)
        scales = []
        if ins:
            whole = dummy.at[pl.ds(0, len(ins) * (rows + 1))]
            pltpu.make_async_remote_copy(
                whole, whole, ssem.at[k], rsem.at[TAKER[ins[0]]], device_id=at(dx=1), device_id_type=MESH
            ).wait_recv()
        for n in ins:
            scales.append(jnp.concatenate([hrcv[k][MESSAGES[n][1]]] * 2, axis=1))

        def value(r, size):
            acc = part[b, pl.ds(first + r, size), :]
            for n, scale in zip(ins, scales):
                acc = acc + rcv[k][MESSAGES[n][1], pl.ds(r, size), :].astype(jnp.float32) * scale
            return acc

        if out is None:

            def final(g, total):
                acc = value(g * step, step)
                grad[pl.ds(first + g * step, step), :] = acc
                return total + jnp.sum((acc * acc).reshape(step // 8, 8, 256), axis=0)

            sums = lax.fori_loop(0, rows // step, final, sums)
            continue

        def high(g, top):
            acc = value(g * step, step)
            if ins:
                tmp[pl.ds(g * step, step), :] = acc
            return jnp.maximum(top, jnp.max(jnp.abs(acc).reshape(step // 8, 8, 256), axis=0))

        top = lax.fori_loop(0, rows // step, high, jnp.full((8, 256), TINY, jnp.float32))
        top = jnp.max(jnp.maximum(top[:, :LANES], top[:, LANES:]), axis=0, keepdims=True)
        i = MESSAGES[name][1]
        hsnd[k][i] = top * (1.0 / LIMIT)
        inverse = jnp.concatenate([LIMIT / top] * 2, axis=1)

        def narrow(g, _):
            acc = tmp[pl.ds(g * step, step), :] if ins else part[b, pl.ds(first + g * step, step), :]
            snd[k][i, pl.ds(g * step, step), :] = jnp.round(acc * inverse).astype(jnp.int16)
            return 0

        lax.fori_loop(0, rows // step, narrow, 0)
        if not entered:
            pl.semaphore_wait(barrier, len(peers))
            pl.semaphore_signal(far, inc=1, device_id=at(0, 0, 1, 0), device_id_type=MESH)
            entered = True
        data, head = send(name)
        head.start()
        data.start()

    sums = jnp.sum(sums, axis=0, keepdims=True)
    red[...] = sums[:, :LANES] + sums[:, LANES:]
    zs = [lax.rem(z + d, NZ) * NX for d in range(NZ)]
    xs = [lax.rem(x + d, NX) for d in range(NX)]
    ys = [lax.rem(y + d, NY) * 2 for d in range(NY)]
    cs = [core, 1 - core]
    for j, (dz, dx, dy, dc) in enumerate(others):
        to = {"section": ys[dy] + cs[dc], "dp": zs[dz] + xs[dx]}
        pltpu.make_async_remote_copy(red, heard.at[j], s0, r0, device_id=to, device_id_type=MESH).start()
    for k in range(len(CLASSES)):
        for buf, sem in ((snd[k], ssem.at[k]), (hsnd[k], hssem.at[k])):
            pltpu.make_async_remote_copy(
                buf, buf, sem, rsem.at[0], device_id=at(dx=1), device_id_type=MESH
            ).wait_send()
    for j in range(0, 256, 128):
        turned[j : j + 128, :] = grad[:, j : j + 128].T
    store = pltpu.make_async_copy(turned, g_out, gsem)
    store.start()
    whole = pltpu.make_async_remote_copy(heard, heard, s0, r0, device_id=at(dx=1), device_id_type=MESH)
    fload.wait()
    power_one, power_two = jnp.float32(beta_first), jnp.float32(beta_second)
    for i in range(flags.shape[0]):
        counted = flags[i] == 0
        power_one = power_one * jnp.where(counted, jnp.float32(beta_first), jnp.float32(1.0))
        power_two = power_two * jnp.where(counted, jnp.float32(beta_second), jnp.float32(1.0))
    shape = (1, width)
    scale[1:2, :] = 1.0 / (1.0 - jnp.full(shape, power_one, jnp.float32))
    scale[2:3, :] = 1.0 / (1.0 - jnp.full(shape, power_two, jnp.float32))
    scale[3:8, :] = jnp.zeros((5, width), jnp.float32)
    scale[0:1, LANES:] = jnp.zeros((1, width - LANES), jnp.float32)
    whole.wait_recv()
    scale[0:1, :LANES] = red[...] + jnp.sum(heard[...], axis=0)
    put = pltpu.make_async_copy(scale, scale_out, msem)
    put.start()
    whole.wait_send()
    put.wait()
    store.wait()


def reduced(layer_inputs, key_cotangent, token_counts, flags):
    _, tokens, depth = layer_inputs.shape
    width = key_cotangent.shape[2]
    anywhere = pl.BlockSpec(memory_space=pltpu.HBM)
    pieces = [PIECES[c][1] for c in CLASSES]
    return pl.pallas_call(
        kernel,
        out_shape=(
            jax.ShapeDtypeStruct((256, width), jnp.float32),
            jax.ShapeDtypeStruct((8, width), jnp.float32),
        ),
        in_specs=[anywhere] * 4,
        out_specs=(anywhere, anywhere),
        scratch_shapes=[
            pltpu.VMEM((32, tokens, 256), jnp.bfloat16),
            pltpu.VMEM((tokens, width), jnp.bfloat16),
            pltpu.VMEM((tokens, width), jnp.float32),
            pltpu.VMEM((width, tokens), jnp.bfloat16),
            pltpu.VMEM((32, width, 256), jnp.float32),
            pltpu.VMEM((160, 256), jnp.float32),
            pltpu.VMEM((width, 256), jnp.float32),
            *[pltpu.VMEM((N_MSG, r, 256), jnp.int16) for r in pieces],
            *[pltpu.VMEM((N_MSG, r, 256), jnp.int16) for r in pieces],
            *[pltpu.VMEM((N_MSG, 1, LANES), jnp.float32) for r in pieces],
            *[pltpu.VMEM((N_MSG, 1, LANES), jnp.float32) for r in pieces],
            pltpu.SemaphoreType.DMA((len(CLASSES),)),
            pltpu.SemaphoreType.DMA((max(SLOT) + 1,)),
            pltpu.SemaphoreType.DMA((len(CLASSES),)),
            pltpu.VMEM((4 * 161, 1, LANES), jnp.float32),
            pltpu.SemaphoreType.DMA((len(BLOCKS) // GROUP + 1,)),
            pltpu.SemaphoreType.DMA,
            pltpu.VMEM((1, LANES), jnp.float32),
            pltpu.VMEM((255, 1, LANES), jnp.float32),
            pltpu.SemaphoreType.DMA,
            pltpu.SemaphoreType.DMA,
            pltpu.VMEM((256, width), jnp.float32),
            pltpu.SemaphoreType.DMA,
            pltpu.SemaphoreType.REGULAR,
            pltpu.VMEM((8, width), jnp.float32),
            pltpu.SMEM(token_counts.shape, jnp.int32),
            pltpu.SMEM(flags.shape, jnp.int32),
            pltpu.SemaphoreType.DMA,
            pltpu.SemaphoreType.DMA,
            pltpu.SemaphoreType.REGULAR,
        ],
        compiler_params=pltpu.CompilerParams(
            collective_id=0, has_side_effects=True, vmem_limit_bytes=56 << 20
        ),
    )(layer_inputs, key_cotangent, token_counts, flags)


def update(entries, grad, scale_hbm, param, first, second, *rest):
    outs, held, kept, scale, gsem, sems, ssem = rest[:4], *rest[4:]
    step = kept.shape[1] // STEPS
    get = pltpu.make_async_copy(scale_hbm, scale, ssem)
    get.start()
    parts = [pl.ds(i * step, step) for i in range(STEPS)]
    for i, part in enumerate(parts):
        sources = (grad.at[part], param.at[0, part], first.at[0, part], second.at[0, part])
        for j, source in enumerate(sources):
            pltpu.make_async_copy(source, held.at[j, part], gsem.at[i]).start()
    get.wait()
    unbias_one, unbias_two = scale[1:2, :], scale[2:3, :]
    total_sq = jnp.sum(scale[0:1, :], axis=1, keepdims=True)
    clip_scale = clip_level * math.sqrt(entries) / (jnp.sqrt(total_sq) + 1e-06)
    clip_scale = jnp.broadcast_to(clip_scale, unbias_one.shape)
    for i, part in enumerate(parts):
        pltpu.make_async_copy(held.at[:, part], held.at[:, part], gsem.at[i]).wait()
        clipped = held[0, part, :] * clip_scale
        now = held[1, part, :]
        one = beta_first * held[2, part, :] + (1.0 - beta_first) * clipped
        two = beta_second * held[3, part, :] + (1.0 - beta_second) * clipped * clipped
        turn = one * unbias_one / (jnp.sqrt(two * unbias_two) + adam_epsilon) + weight_decay * now
        for j, value in enumerate((now - learn_rate * turn, one, two, turn)):
            kept[j, part, :] = value
            pltpu.make_async_copy(kept.at[j, part], outs[j].at[0, part], sems.at[j]).start()
    for j in range(4):
        pltpu.make_async_copy(kept.at[j], outs[j].at[0], sems.at[j]).wait()


def local(
    layer_inputs,
    key_cotangent,
    token_counts,
    rollback_flags,
    master_param,
    first_moment,
    second_moment,
):
    _, shard_rows, width = master_param.shape
    entries = lax.axis_size("section") * lax.axis_size("dp") * shard_rows * width
    gradient, scale = reduced(layer_inputs, key_cotangent, token_counts, rollback_flags)
    anywhere = pl.BlockSpec(memory_space=pltpu.HBM)
    return pl.pallas_call(
        functools.partial(update, entries),
        out_shape=(jax.ShapeDtypeStruct(master_param.shape, jnp.float32),) * 4,
        in_specs=(anywhere,) * 5,
        out_specs=(anywhere,) * 4,
        scratch_shapes=[
            pltpu.VMEM((4, shard_rows, width), jnp.float32),
            pltpu.VMEM((4, shard_rows, width), jnp.float32),
            pltpu.VMEM((8, width), jnp.float32),
            pltpu.SemaphoreType.DMA((STEPS,)),
            pltpu.SemaphoreType.DMA((4,)),
            pltpu.SemaphoreType.DMA,
        ],
        compiler_params=pltpu.CompilerParams(vmem_limit_bytes=60 << 20),
        cost_estimate=pl.CostEstimate(flops=20 << 17, bytes_accessed=4 << 20, transcendentals=1 << 17),
    )(gradient, scale, master_param, first_moment, second_moment)


def solution(mesh):
    placed = (
        P("section", "dp", None),
        P("section", "dp", None),
        P("dp", None),
        P(),
        P("section", "dp", None),
        P("section", "dp", None),
        P("section", "dp", None),
    )
    return jax.shard_map(
        local,
        mesh=mesh,
        in_specs=placed,
        out_specs=(P("section", "dp", None),) * 4,
        check_vma=False,
    )
```
